512 devices in a mesh: dp: 16 (over z_lo, y), seq: 32 (over z_hi, x, core).
Axes of the slice: x: 4, y: 8, z: 8 (z_hi: 4, z_lo: 2; z = z_hi * 2 + z_lo), core: 2. Of those that a mesh axis runs over, the one named last changes fastest.
Arguments:
- latents: bfloat16 [512, 16, 16384], P('dp', None, 'seq'), may hold values from -8 to 8, as said below
- noise: bfloat16 [512, 16, 16384], P('dp', None, 'seq'), may hold values from -6 to 6
Outputs:
- targets: bfloat16 [512, 16, 16384], P('dp', None, 'seq')
- row_potential: float32 [512], replicated
- column_potential: float32 [512], P('dp')
The draws below stay inside these ranges and needn't reach their ends.
Inputs may be any that keep to these rules, and one draw needn't show every extreme that they name: `latents`: each clip's values have a clip-dependent scale.
All inputs are finite; a program needn't handle non-finite values.
Results may differ from the reference program's by a relative error of at most 0.0065.
Values may be sent and summed in bfloat16 or wider, within the bound.
No kernel may reach another device: no remote copies, remote signals or barrier semaphores. Data moves between devices by JAX's collectives and lax.ppermute only.
A program may use at most 64 MiB of HBM per device.

```python
import math
import jax
import jax.numpy as jnp
from jax import lax

CH = 16
ITERS = 4
CLIPS = 512
POSITIONS = 16384


def draw_latents(key, part):
    key = jax.random.fold_in(key, 11)
    scale_key, value_key = jax.random.split(key, 2)
    scales = jnp.exp(jax.random.uniform(scale_key, (CLIPS, 1, 1), jnp.float32, math.log(0.5), math.log(2.0)))
    values = jax.random.truncated_normal(value_key, -4.0, 4.0, (CLIPS, CH, POSITIONS), jnp.float32)
    return (scales * values).astype(jnp.bfloat16)


def level_of(key, extent, cuts, low, high):
    loudness = 1.0
    for axis_at, blocks in cuts:
        steps = jax.random.uniform(jax.random.fold_in(jax.random.fold_in(key, 6), axis_at), (blocks,), jnp.float32, low / len(cuts), high / len(cuts))
        loudness = loudness * jnp.repeat(jnp.exp(steps), extent[axis_at] // blocks).reshape((-1,) + (1,) * (len(extent) - 1 - axis_at))
    return loudness


def normal_values(rng, dims, spread, bound, pieces=(), kind=jnp.bfloat16):
    result = spread * jax.random.normal(rng, dims, jnp.float32)
    if pieces:
        result = result * level_of(rng, dims, pieces, -0.22, 0.18)
    return jnp.clip(result, -bound, bound).astype(kind)


def setup_inputs(seed: int = 0) -> dict:
    key_of = jax.random.split(jax.random.key(seed), 3)
    return {
        "latents": draw_latents(jax.random.fold_in(key_of[2], 71), 0),
        "noise": normal_values(key_of[1], (CLIPS, CH, POSITIONS), 1.0, 6.0, ((0, 16), (2, 32))),
    }


blur = 0.5

def log_sum(values, axis):
    top = lax.optimization_barrier(jnp.max(values, axis=axis, keepdims=True))
    return jnp.squeeze(top, axis) + jnp.log(lax.optimization_barrier(jnp.sum(jnp.exp(values - top), axis=axis)))

def reference(latents, noise):
    flat_latents = latents.reshape(CLIPS, CH * POSITIONS)
    flat_noise = noise.reshape(CLIPS, CH * POSITIONS)
    cross = jnp.dot(flat_noise, flat_latents.T, preferred_element_type=jnp.float32)
    noise_norms = lax.optimization_barrier(jnp.sum(jnp.square(flat_noise.astype(jnp.float32)), axis=1))
    latent_norms = lax.optimization_barrier(jnp.sum(jnp.square(flat_latents.astype(jnp.float32)), axis=1))
    summed = noise_norms[:, None] + latent_norms[None, :] - 2.0 * cross
    cost = summed / math.sqrt(CH * POSITIONS)
    log_mass = -math.log(CLIPS)
    row_potential = jnp.zeros((CLIPS,), jnp.float32)
    column_potential = jnp.zeros((CLIPS,), jnp.float32)
    for step in range(ITERS):
        column_potential = blur * log_mass - blur * log_sum((row_potential[:, None] - cost) / blur, 0)
        row_potential = blur * log_mass - blur * log_sum((column_potential[None, :] - cost) / blur, 1)
    plan = jnp.exp((row_potential[:, None] + column_potential[None, :] - cost) / blur)
    weights = (plan / lax.optimization_barrier(jnp.sum(plan, axis=0))[None, :]).astype(jnp.bfloat16)
    moved = jnp.dot(weights.T, flat_noise, preferred_element_type=jnp.float32)
    targets = moved.astype(jnp.bfloat16).reshape(CLIPS, CH, POSITIONS)
    return (targets, row_potential, column_potential)
```

```python
import functools
import math

import jax
import jax.numpy as jnp
from jax import lax
from jax.experimental import pallas as pl
from jax.experimental.pallas import tpu as pltpu
from jax.sharding import PartitionSpec as P

ITERS = 4
BLUR = 0.5
CORES = 2
VMEM = pl.BlockSpec(memory_space=pltpu.VMEM)
SMEM = pl.BlockSpec(memory_space=pltpu.SMEM)
LIMIT = pltpu.CompilerParams(vmem_limit_bytes=32 * 1024 * 1024)


def pair_kernel(core_ref, clips_ref, send_ref, keep_ref):
    sources, both, width = clips_ref.shape
    local = both // 2
    half = sources // CORES
    core = core_ref[0]
    noise = clips_ref[:, :local, :].reshape(sources * local, width)
    wide = noise.astype(jnp.float32)
    noise_norms = jnp.sum(wide * wide, axis=1, keepdims=True)
    for first, out_ref in ((half * (1 - core), send_ref), (half * core, keep_ref)):
        latents = clips_ref[pl.ds(first, half), local:, :].reshape(half * local, width)
        wide = latents.astype(jnp.float32)
        latent_norms = jnp.sum(wide * wide, axis=1, keepdims=True)
        latent_norms = jnp.transpose(jnp.broadcast_to(latent_norms, (half * local, 128)))[:1, :]
        cross = lax.dot_general(
            noise, latents, (((1,), (1,)), ((), ())), preferred_element_type=jnp.float32
        )
        out_ref[...] = noise_norms + latent_norms - 2.0 * cross


def spread_kernel(parts_ref, out_ref):
    out_ref[...] = jnp.broadcast_to(jnp.sum(parts_ref[...], axis=0)[None], out_ref.shape)


def coupling_kernel(factor, core_ref, own_ref, other_ref, clips_ref, moved_ref, row_ref, column_ref, *scores):
    sources, both, width = clips_ref.shape
    local = both // 2
    core = core_ref[0]
    total = sources * local
    log_mass = -math.log2(total)
    for score, given in zip(scores, (own_ref, other_ref), strict=True):
        score[...] = given[...] * factor
    row = jnp.zeros((total, 1), jnp.float32)
    columns = [None] * CORES
    for step in range(ITERS):
        for k, score in enumerate(scores):
            value = row - score[...]
            top = jnp.max(value, axis=0, keepdims=True)
            mass = jnp.sum(jnp.exp2(value - top), axis=0, keepdims=True)
            columns[k] = log_mass - (top + jnp.log2(mass))
        values = [column - score[...] for column, score in zip(columns, scores, strict=True)]
        top = jnp.max(jnp.maximum(*values), axis=1, keepdims=True)
        mass = jnp.sum(sum(jnp.exp2(value - top) for value in values), axis=1, keepdims=True)
        row = log_mass - (top + jnp.log2(mass))
    noise = clips_ref[:, :local, :].reshape(total, width)
    back = BLUR * math.log(2.0)
    row_ref[...] = jnp.transpose(jnp.broadcast_to(row * back, (total, 128)))[:8, :]
    for k, (column, score) in enumerate(zip(columns, scores, strict=True)):
        place = core if k == 0 else 1 - core
        plan = jnp.exp2((row + column) - score[...])
        weights = (plan / jnp.sum(plan, axis=0, keepdims=True)).astype(jnp.bfloat16)
        moved = lax.dot_general(
            weights, noise, (((0,), (0,)), ((), ())), preferred_element_type=jnp.float32
        )
        moved_ref[place] = moved.astype(jnp.bfloat16)
        column_ref[place] = jnp.broadcast_to(column * back, column_ref.shape[1:])


def per_device(latents, noise):
    local, channels, width = latents.shape
    dp, seq = lax.axis_size("dp"), lax.axis_size("seq")
    total = local * dp
    half = total // CORES
    factor = math.log2(math.e) / (BLUR * math.sqrt(channels * width * seq))
    core = lax.rem(lax.axis_index("seq"), CORES)
    core_scalar = core.reshape(1).astype(jnp.int32)
    swap = [(i, i ^ 1) for i in range(seq)]
    chips = [list(range(c, seq, CORES)) for c in range(CORES)]

    packed = jnp.concatenate([noise, latents], axis=0).swapaxes(0, 1)
    clips = lax.all_to_all(packed, "dp", 0, 0, tiled=True)

    block = jax.ShapeDtypeStruct((total, half), jnp.float32)
    send, keep = pl.pallas_call(
        pair_kernel,
        out_shape=(block, block),
        in_specs=[SMEM, VMEM],
        out_specs=(VMEM, VMEM),
        compiler_params=LIMIT,
    )(core_scalar, clips)
    summed = keep + lax.ppermute(send, "seq", swap)

    spread = pl.pallas_call(
        spread_kernel,
        out_shape=jax.ShapeDtypeStruct((dp, local, half), jnp.float32),
        in_specs=[VMEM],
        out_specs=VMEM,
        compiler_params=LIMIT,
    )
    parts = lax.all_to_all(summed.reshape(dp, local, half), "dp", 0, 0, tiled=True)
    parts = lax.all_to_all(spread(parts), "seq", 0, 0, tiled=True, axis_index_groups=chips)
    own = lax.all_to_all(spread(parts), "dp", 0, 0, tiled=True).reshape(total, half)
    other = lax.ppermute(own, "seq", swap)

    moved, row, column = pl.pallas_call(
        functools.partial(coupling_kernel, factor),
        out_shape=(
            jax.ShapeDtypeStruct((CORES, half, width), jnp.bfloat16),
            jax.ShapeDtypeStruct((8, total), jnp.float32),
            jax.ShapeDtypeStruct((CORES, 8, half), jnp.float32),
        ),
        in_specs=[SMEM, VMEM, VMEM, VMEM],
        out_specs=(VMEM, VMEM, VMEM),
        scratch_shapes=[pltpu.VMEM((total, half), jnp.float32)] * CORES,
        compiler_params=LIMIT,
    )(core_scalar, own, other, clips)
    back = lax.all_to_all(moved.reshape(dp, local, width), "dp", 0, 0, tiled=True)
    targets = back.swapaxes(0, 1)
    column = lax.dynamic_slice(
        column[:, 0, :].reshape(total), (lax.axis_index("dp") * local,), (local,)
    )
    return (targets, row[0], column)


def solution(mesh):
    in_specs = (P("dp", None, "seq"), P("dp", None, "seq"))
    out_specs = (P("dp", None, "seq"), P(), P("dp"))
    return jax.shard_map(
        per_device, mesh=mesh, in_specs=in_specs, out_specs=out_specs, check_vma=False
    )
```

```python
import functools
import math

import jax
import jax.numpy as jnp
from jax import lax
from jax.experimental import pallas as pl
from jax.experimental.pallas import tpu as pltpu
from jax.sharding import Mesh, PartitionSpec as P

ITERS = 4
BLUR = 0.5
CORES = 2
FINE = {"z": 2, "q": 4, "p": 2, "h": 4, "x": 4, "c": 2}
DP = ("z", "q", "p")
SEQ = ("h", "x", "c")
NEAR = ("x", "z", "p")
VMEM = pl.BlockSpec(memory_space=pltpu.VMEM)
SMEM = pl.BlockSpec(memory_space=pltpu.SMEM)
LIMIT = pltpu.CompilerParams(vmem_limit_bytes=32 * 1024 * 1024)


def pack_kernel(noise_ref, latents_ref, out_ref):
    local = noise_ref.shape[0]
    out_ref[:, :local, :] = jnp.swapaxes(noise_ref[...], 0, 1)
    out_ref[:, local:, :] = jnp.swapaxes(latents_ref[...], 0, 1)


def pair_kernel(core_ref, clips_ref, send_ref, keep_ref):
    sources, both, width = clips_ref.shape
    local = both // 2
    half = sources // CORES
    core = core_ref[0]
    noise = clips_ref[:, :local, :].reshape(sources * local, width)
    wide = noise.astype(jnp.float32)
    noise_norms = jnp.sum(wide * wide, axis=1, keepdims=True)
    for first, out_ref in ((half * (1 - core), send_ref), (half * core, keep_ref)):
        latents = clips_ref[pl.ds(first, half), local:, :].reshape(half * local, width)
        wide = latents.astype(jnp.float32)
        latent_norms = jnp.sum(wide * wide, axis=1, keepdims=True)
        latent_norms = jnp.transpose(jnp.broadcast_to(latent_norms, (half * local, 128)))[:1, :]
        cross = lax.dot_general(
            noise, latents, (((1,), (1,)), ((), ())), preferred_element_type=jnp.float32
        )
        out_ref[...] = noise_norms + latent_norms - 2.0 * cross


def spread_kernel(parts_ref, out_ref):
    out_ref[...] = jnp.broadcast_to(jnp.sum(parts_ref[...], axis=0)[None], out_ref.shape)


def spread(parts, copies):
    return pl.pallas_call(
        spread_kernel,
        out_shape=jax.ShapeDtypeStruct((copies, *parts.shape[1:]), parts.dtype),
        in_specs=[VMEM],
        out_specs=VMEM,
        compiler_params=LIMIT,
    )(parts)


def exchange(blocks, axes):
    return lax.all_to_all(blocks, axes, 0, 0, tiled=True)


def coupling_kernel(factor, core_ref, own_ref, other_ref, clips_ref, moved_ref, row_ref, column_ref, *scores):
    sources, both, width = clips_ref.shape
    local = both // 2
    core = core_ref[0]
    total = sources * local
    log_mass = -math.log2(total)
    for score, given in zip(scores, (own_ref, other_ref), strict=True):
        score[...] = given[...] * factor
    row = jnp.zeros((total, 1), jnp.float32)
    columns = [None] * CORES
    for step in range(ITERS):
        for k, score in enumerate(scores):
            value = row - score[...]
            top = jnp.max(value, axis=0, keepdims=True)
            mass = jnp.sum(jnp.exp2(value - top), axis=0, keepdims=True)
            columns[k] = log_mass - (top + jnp.log2(mass))
        values = [column - score[...] for column, score in zip(columns, scores, strict=True)]
        top = jnp.max(jnp.maximum(*values), axis=1, keepdims=True)
        mass = jnp.sum(sum(jnp.exp2(value - top) for value in values), axis=1, keepdims=True)
        row = log_mass - (top + jnp.log2(mass))
    noise = clips_ref[:, :local, :].reshape(total, width)
    back = BLUR * math.log(2.0)
    row_ref[...] = jnp.transpose(jnp.broadcast_to(row * back, (total, 128)))[:8, :]
    for k, (column, score) in enumerate(zip(columns, scores, strict=True)):
        place = core if k == 0 else 1 - core
        plan = jnp.exp2((row + column) - score[...])
        weights = (plan / jnp.sum(plan, axis=0, keepdims=True)).astype(jnp.bfloat16)
        moved = lax.dot_general(
            weights, noise, (((0,), (0,)), ((), ())), preferred_element_type=jnp.float32
        )
        moved_ref[place] = moved.astype(jnp.bfloat16)
        column_ref[place] = jnp.broadcast_to(column * back, column_ref.shape[1:])


def per_device(latents, noise):
    local, channels, width = latents.shape
    dp, seq, near = lax.axis_size(DP), lax.axis_size(SEQ), lax.axis_size(NEAR)
    total = local * dp
    half = total // CORES
    factor = math.log2(math.e) / (BLUR * math.sqrt(channels * width * seq))
    core = lax.axis_index("c").reshape(1).astype(jnp.int32)
    swap = [(0, 1), (1, 0)]

    packed = pl.pallas_call(
        pack_kernel,
        out_shape=jax.ShapeDtypeStruct((channels, 2 * local, width), noise.dtype),
        in_specs=[VMEM, VMEM],
        out_specs=VMEM,
        compiler_params=LIMIT,
    )(noise, latents)
    clips = exchange(packed, DP)

    block = jax.ShapeDtypeStruct((total, half), jnp.float32)
    send, keep = pl.pallas_call(
        pair_kernel,
        out_shape=(block, block),
        in_specs=[SMEM, VMEM],
        out_specs=(VMEM, VMEM),
        compiler_params=LIMIT,
    )(core, clips)
    summed = keep + lax.ppermute(send, "c", swap)

    parts = exchange(summed.reshape(near, total // near, half), NEAR)
    parts = exchange(spread(parts, lax.axis_size("h")), "h")
    parts = exchange(spread(parts, lax.axis_size("q")), "q")
    own = exchange(spread(parts, near), NEAR).reshape(total, half)
    other = lax.ppermute(own, "c", swap)

    moved, row, column = pl.pallas_call(
        functools.partial(coupling_kernel, factor),
        out_shape=(
            jax.ShapeDtypeStruct((CORES, half, width), jnp.bfloat16),
            jax.ShapeDtypeStruct((8, total), jnp.float32),
            jax.ShapeDtypeStruct((CORES, 8, half), jnp.float32),
        ),
        in_specs=[SMEM, VMEM, VMEM, VMEM],
        out_specs=(VMEM, VMEM, VMEM),
        scratch_shapes=[pltpu.VMEM((total, half), jnp.float32)] * CORES,
        compiler_params=LIMIT,
    )(core, own, other, clips)
    targets = exchange(moved.reshape(dp, local, width), DP).swapaxes(0, 1)
    column = lax.dynamic_slice(
        column[:, 0, :].reshape(total), (lax.axis_index(DP) * local,), (local,)
    )
    return (targets, row[0], column)


def solution(mesh):
    fine = Mesh(mesh.devices.reshape(tuple(FINE.values())), tuple(FINE))
    in_specs = (P(DP, None, SEQ), P(DP, None, SEQ))
    out_specs = (P(DP, None, SEQ), P(), P(DP))
    return jax.shard_map(
        per_device, mesh=fine, in_specs=in_specs, out_specs=out_specs, check_vma=False
    )
```

```python
import functools
import math

import jax
import jax.numpy as jnp
from jax import lax
from jax.experimental import pallas as pl
from jax.experimental.pallas import tpu as pltpu
from jax.sharding import Mesh, PartitionSpec as P

ITERS = 4
BLUR = 0.5
CORES = 2
FINE = {"z": 2, "q": 4, "p": 2, "h": 4, "x": 4, "c": 2}
DP = ("z", "q", "p")
SEQ = ("h", "x", "c")
NEAR = ("x", "z", "p")
ANY = pl.BlockSpec(memory_space=pl.ANY)
VMEM = pl.BlockSpec(memory_space=pltpu.VMEM)
SMEM = pl.BlockSpec(memory_space=pltpu.SMEM)
WHOLE = pltpu.CompilerParams(vmem_limit_bytes=60 * 1024 * 1024)
LIMIT = pltpu.CompilerParams(vmem_limit_bytes=32 * 1024 * 1024)


def pack_kernel(noise_ref, latents_ref, out_ref, held, arrived):
    local = noise_ref.shape[0]
    copies = [
        pltpu.make_async_copy(given, held.at[k], arrived.at[k])
        for k, given in enumerate((noise_ref, latents_ref))
    ]
    for copy in copies:
        copy.start()
    for k, copy in enumerate(copies):
        copy.wait()
        out_ref[:, k * local : (k + 1) * local, :] = jnp.swapaxes(held[k], 0, 1)


def pair_kernel(core_ref, clips_ref, send_ref, keep_ref):
    sources, both, width = clips_ref.shape
    local = both // 2
    half = sources // CORES
    core = core_ref[0]
    noise = clips_ref[:, :local, :].reshape(sources * local, width)
    wide = noise.astype(jnp.float32)
    noise_norms = jnp.sum(wide * wide, axis=1, keepdims=True)
    for first, out_ref in ((half * (1 - core), send_ref), (half * core, keep_ref)):
        latents = clips_ref[pl.ds(first, half), local:, :].reshape(half * local, width)
        wide = latents.astype(jnp.float32)
        latent_norms = jnp.sum(wide * wide, axis=1, keepdims=True)
        latent_norms = jnp.transpose(jnp.broadcast_to(latent_norms, (half * local, 128)))[:1, :]
        cross = lax.dot_general(
            noise, latents, (((1,), (1,)), ((), ())), preferred_element_type=jnp.float32
        )
        out_ref[...] = noise_norms + latent_norms - 2.0 * cross


def spread_kernel(parts_ref, out_ref):
    out_ref[...] = jnp.broadcast_to(jnp.sum(parts_ref[...], axis=0)[None], out_ref.shape)


def spread(parts, copies):
    return pl.pallas_call(
        spread_kernel,
        out_shape=jax.ShapeDtypeStruct((copies, *parts.shape[1:]), parts.dtype),
        in_specs=[VMEM],
        out_specs=VMEM,
        compiler_params=LIMIT,
    )(parts)


def exchange(blocks, axes):
    return lax.all_to_all(blocks, axes, 0, 0, tiled=True)


def coupling_kernel(factor, core_ref, group_ref, own_ref, other_ref, clips_ref, moved_ref, row_ref, column_ref, *scores):
    sources, both, width = clips_ref.shape
    local = both // 2
    core = core_ref[0]
    total = sources * local
    log_mass = -math.log2(total)
    for score, given in zip(scores, (own_ref, other_ref), strict=True):
        score[...] = given[...] * factor
    row = jnp.zeros((total, 1), jnp.float32)
    columns = [None] * CORES
    for step in range(ITERS):
        for k, score in enumerate(scores):
            value = row - score[...]
            top = jnp.max(value, axis=0, keepdims=True)
            mass = jnp.sum(jnp.exp2(value - top), axis=0, keepdims=True)
            columns[k] = log_mass - (top + jnp.log2(mass))
        values = [column - score[...] for column, score in zip(columns, scores, strict=True)]
        top = jnp.max(jnp.maximum(*values), axis=1, keepdims=True)
        mass = jnp.sum(sum(jnp.exp2(value - top) for value in values), axis=1, keepdims=True)
        row = log_mass - (top + jnp.log2(mass))
    noise = clips_ref[:, :local, :].reshape(total, width)
    back = BLUR * math.log(2.0)
    row_ref[...] = jnp.transpose(jnp.broadcast_to(row * back, (total, 128)))[:1, :]
    group = group_ref[0]
    half = total // CORES
    column = jnp.where(group * local // half == core, *columns) * back
    column = pltpu.roll(column, lax.rem(half - lax.rem(group * local, half), half), 1)
    column_ref[...] = column[:, :local]
    for k, (column, score) in enumerate(zip(columns, scores, strict=True)):
        place = core if k == 0 else 1 - core
        plan = jnp.exp2((row + column) - score[...])
        weights = (plan / jnp.sum(plan, axis=0, keepdims=True)).astype(jnp.bfloat16)
        moved = lax.dot_general(
            weights, noise, (((0,), (0,)), ((), ())), preferred_element_type=jnp.float32
        )
        moved_ref[place] = moved.astype(jnp.bfloat16)


def per_device(latents, noise):
    local, channels, width = latents.shape
    dp, seq, near = lax.axis_size(DP), lax.axis_size(SEQ), lax.axis_size(NEAR)
    total = local * dp
    half = total // CORES
    factor = math.log2(math.e) / (BLUR * math.sqrt(channels * width * seq))
    core = lax.axis_index("c").reshape(1).astype(jnp.int32)
    group = lax.axis_index(DP).reshape(1).astype(jnp.int32)
    swap = [(0, 1), (1, 0)]

    packed = pl.pallas_call(
        pack_kernel,
        out_shape=jax.ShapeDtypeStruct((channels, 2 * local, width), noise.dtype),
        in_specs=[ANY, ANY],
        out_specs=VMEM,
        scratch_shapes=[
            pltpu.VMEM((2, *noise.shape), noise.dtype),
            pltpu.SemaphoreType.DMA((2,)),
        ],
        compiler_params=WHOLE,
    )(noise, latents)
    packed, core, group = lax.optimization_barrier((packed, core, group))
    clips = exchange(packed, DP)

    block = jax.ShapeDtypeStruct((total, half), jnp.float32)
    send, keep = pl.pallas_call(
        pair_kernel,
        out_shape=(block, block),
        in_specs=[SMEM, VMEM],
        out_specs=(VMEM, VMEM),
        compiler_params=LIMIT,
    )(core, clips)
    summed = keep + lax.ppermute(send, "c", swap)

    parts = exchange(summed.reshape(near, total // near, half), NEAR)
    parts = exchange(spread(parts, lax.axis_size("h")), "h")
    parts = exchange(spread(parts, lax.axis_size("q")), "q")
    own = exchange(spread(parts, near), NEAR).reshape(total, half)
    other = lax.ppermute(own, "c", swap)

    moved, row, column = pl.pallas_call(
        functools.partial(coupling_kernel, factor),
        out_shape=(
            jax.ShapeDtypeStruct((CORES, half, width), jnp.bfloat16),
            jax.ShapeDtypeStruct((1, total), jnp.float32),
            jax.ShapeDtypeStruct((1, local), jnp.float32),
        ),
        in_specs=[SMEM, SMEM, VMEM, VMEM, VMEM],
        out_specs=(VMEM, VMEM, VMEM),
        scratch_shapes=[pltpu.VMEM((total, half), jnp.float32)] * CORES,
        compiler_params=LIMIT,
    )(core, group, own, other, clips)
    targets = exchange(moved.reshape(dp, local, width), DP).swapaxes(0, 1)
    return (targets, row.reshape(total), column.reshape(local))


def solution(mesh):
    fine = Mesh(mesh.devices.reshape(tuple(FINE.values())), tuple(FINE))
    in_specs = (P(DP, None, SEQ), P(DP, None, SEQ))
    out_specs = (P(DP, None, SEQ), P(), P(DP))
    return jax.shard_map(
        per_device, mesh=fine, in_specs=in_specs, out_specs=out_specs, check_vma=False
    )
```

```python
import functools
import math

import jax
import jax.numpy as jnp
from jax import lax
from jax.experimental import pallas as pl
from jax.experimental.pallas import tpu as pltpu
from jax.sharding import Mesh, PartitionSpec as P

ITERS = 4
BLUR = 0.5
CORES = 2
FINE = {"z": 2, "q": 4, "p": 2, "h": 4, "x": 4, "c": 2}
DP = ("z", "q", "p")
SEQ = ("h", "x", "c")
NEAR = ("x", "z", "p")
HBM = pl.BlockSpec(memory_space=pltpu.HBM)
VMEM = pl.BlockSpec(memory_space=pltpu.VMEM)
SMEM = pl.BlockSpec(memory_space=pltpu.SMEM)
LIMIT = pltpu.CompilerParams(vmem_limit_bytes=32 * 1024 * 1024)


def pack_kernel(noise_ref, latents_ref, out_ref, held, arrived):
    local = noise_ref.shape[0]
    copies = [
        pltpu.make_async_copy(given, held.at[k], arrived.at[k])
        for k, given in enumerate((noise_ref, latents_ref))
    ]
    for copy in copies:
        copy.start()
    for k, copy in enumerate(copies):
        copy.wait()
        out_ref[:, k * local : (k + 1) * local, :] = jnp.swapaxes(held[k], 0, 1)


def pair_kernel(core_ref, clips_ref, send_ref, keep_ref):
    sources, both, width = clips_ref.shape
    local = both // 2
    half = sources // CORES
    core = core_ref[0]
    noise = clips_ref[:, :local, :].reshape(sources * local, width)
    wide = noise.astype(jnp.float32)
    noise_norms = jnp.sum(wide * wide, axis=1, keepdims=True)
    for first, out_ref in ((half * (1 - core), send_ref), (half * core, keep_ref)):
        latents = clips_ref[pl.ds(first, half), local:, :].reshape(half * local, width)
        wide = latents.astype(jnp.float32)
        latent_norms = jnp.sum(wide * wide, axis=1, keepdims=True)
        latent_norms = jnp.transpose(jnp.broadcast_to(latent_norms, (half * local, 128)))[:1, :]
        cross = lax.dot_general(
            noise, latents, (((1,), (1,)), ((), ())), preferred_element_type=jnp.float32
        )
        out_ref[...] = noise_norms + latent_norms - 2.0 * cross


def spread_kernel(parts_ref, out_ref):
    out_ref[...] = jnp.broadcast_to(jnp.sum(parts_ref[...], axis=0)[None], out_ref.shape)


def spread(parts, copies):
    return pl.pallas_call(
        spread_kernel,
        out_shape=jax.ShapeDtypeStruct((copies, *parts.shape[1:]), parts.dtype),
        in_specs=[VMEM],
        out_specs=VMEM,
        compiler_params=LIMIT,
    )(parts)


def exchange(blocks, axes):
    return lax.all_to_all(blocks, axes, 0, 0, tiled=True)


def coupling_kernel(factor, core_ref, group_ref, own_ref, other_ref, clips_ref, moved_ref, row_ref, column_ref, *scores):
    sources, both, width = clips_ref.shape
    local = both // 2
    core = core_ref[0]
    total = sources * local
    log_mass = -math.log2(total)
    for score, given in zip(scores, (own_ref, other_ref), strict=True):
        score[...] = given[...] * factor
    row = jnp.zeros((total, 1), jnp.float32)
    columns = [None] * CORES
    for step in range(ITERS):
        for k, score in enumerate(scores):
            value = row - score[...]
            top = jnp.max(value, axis=0, keepdims=True)
            mass = jnp.sum(jnp.exp2(value - top), axis=0, keepdims=True)
            columns[k] = log_mass - (top + jnp.log2(mass))
        values = [column - score[...] for column, score in zip(columns, scores, strict=True)]
        top = jnp.max(jnp.maximum(*values), axis=1, keepdims=True)
        mass = jnp.sum(sum(jnp.exp2(value - top) for value in values), axis=1, keepdims=True)
        row = log_mass - (top + jnp.log2(mass))
    noise = clips_ref[:, :local, :].reshape(total, width)
    back = BLUR * math.log(2.0)
    row_ref[...] = jnp.transpose(jnp.broadcast_to(row * back, (total, 128)))[:1, :]
    group = group_ref[0]
    half = total // CORES
    column = jnp.where(group * local // half == core, *columns) * back
    column = pltpu.roll(column, lax.rem(half - lax.rem(group * local, half), half), 1)
    column_ref[...] = column[:, :local]
    for k, (column, score) in enumerate(zip(columns, scores, strict=True)):
        place = core if k == 0 else 1 - core
        plan = jnp.exp2((row + column) - score[...])
        weights = (plan / jnp.sum(plan, axis=0, keepdims=True)).astype(jnp.bfloat16)
        moved = lax.dot_general(
            weights, noise, (((0,), (0,)), ((), ())), preferred_element_type=jnp.float32
        )
        moved_ref[place] = moved.astype(jnp.bfloat16)


def per_device(latents, noise):
    local, channels, width = latents.shape
    dp, seq, near = lax.axis_size(DP), lax.axis_size(SEQ), lax.axis_size(NEAR)
    total = local * dp
    half = total // CORES
    factor = math.log2(math.e) / (BLUR * math.sqrt(channels * width * seq))
    core = lax.axis_index("c").reshape(1).astype(jnp.int32)
    group = lax.axis_index(DP).reshape(1).astype(jnp.int32)
    swap = [(0, 1), (1, 0)]

    packed = pl.pallas_call(
        pack_kernel,
        out_shape=jax.ShapeDtypeStruct((channels, 2 * local, width), noise.dtype),
        in_specs=[HBM, HBM],
        out_specs=VMEM,
        scratch_shapes=[
            pltpu.VMEM((2, *noise.shape), noise.dtype),
            pltpu.SemaphoreType.DMA((2,)),
        ],
        compiler_params=LIMIT,
    )(noise, latents)
    packed, core, group = lax.optimization_barrier((packed, core, group))
    clips = exchange(packed, DP)

    block = jax.ShapeDtypeStruct((total, half), jnp.float32)
    send, keep = pl.pallas_call(
        pair_kernel,
        out_shape=(block, block),
        in_specs=[SMEM, VMEM],
        out_specs=(VMEM, VMEM),
        compiler_params=LIMIT,
    )(core, clips)
    summed = keep + lax.ppermute(send, "c", swap)

    parts = exchange(summed.reshape(near, total // near, half), NEAR)
    parts = exchange(spread(parts, lax.axis_size("h")), "h")
    parts = exchange(spread(parts, lax.axis_size("q")), "q")
    own = exchange(spread(parts, near), NEAR).reshape(total, half)
    other = lax.ppermute(own, "c", swap)

    moved, row, column = pl.pallas_call(
        functools.partial(coupling_kernel, factor),
        out_shape=(
            jax.ShapeDtypeStruct((CORES, half, width), jnp.bfloat16),
            jax.ShapeDtypeStruct((1, total), jnp.float32),
            jax.ShapeDtypeStruct((1, local), jnp.float32),
        ),
        in_specs=[SMEM, SMEM, VMEM, VMEM, VMEM],
        out_specs=(VMEM, VMEM, VMEM),
        scratch_shapes=[pltpu.VMEM((total, half), jnp.float32)] * CORES,
        compiler_params=LIMIT,
    )(core, group, own, other, clips)
    targets = exchange(moved.reshape(dp, local, width), DP).swapaxes(0, 1)
    return (targets, row.reshape(total), column.reshape(local))


def solution(mesh):
    fine = Mesh(mesh.devices.reshape(tuple(FINE.values())), tuple(FINE))
    in_specs = (P(DP, None, SEQ), P(DP, None, SEQ))
    out_specs = (P(DP, None, SEQ), P(), P(DP))
    return jax.shard_map(
        per_device, mesh=fine, in_specs=in_specs, out_specs=out_specs, check_vma=False
    )
```

```python
import functools
import math

import jax
import jax.numpy as jnp
from jax import lax
from jax.experimental import pallas as pl
from jax.experimental.pallas import tpu as pltpu
from jax.sharding import Mesh, PartitionSpec as P

ITERS = 4
BLUR = 0.5
CORES = 2
FINE = {"z": 2, "q": 4, "p": 2, "h": 4, "x": 4, "c": 2}
DP = ("z", "q", "p")
SEQ = ("h", "x", "c")
NEAR = ("x", "z", "p")
HBM = pl.BlockSpec(memory_space=pltpu.HBM)
VMEM = pl.BlockSpec(memory_space=pltpu.VMEM)
SMEM = pl.BlockSpec(memory_space=pltpu.SMEM)
LIMIT = pltpu.CompilerParams(vmem_limit_bytes=32 * 1024 * 1024)


def pack_kernel(noise_ref, latents_ref, out_ref, held, arrived):
    local = noise_ref.shape[0]
    copies = [
        pltpu.make_async_copy(given, held.at[k], arrived.at[k])
        for k, given in enumerate((noise_ref, latents_ref))
    ]
    for copy in copies:
        copy.start()
    for k, copy in enumerate(copies):
        copy.wait()
        out_ref[:, k * local : (k + 1) * local, :] = jnp.swapaxes(held[k], 0, 1)


def pair_kernel(factor, core_ref, clips_ref, send_ref, keep_ref):
    sources, both, width = clips_ref.shape
    local = both // 2
    half = sources // CORES
    core = core_ref[0]
    noise = clips_ref[:, :local, :].reshape(sources * local, width)
    wide = noise.astype(jnp.float32)
    noise_norms = jnp.sum(wide * wide, axis=1, keepdims=True) * factor
    for first, out_ref in ((half * (1 - core), send_ref), (half * core, keep_ref)):
        latents = clips_ref[pl.ds(first, half), local:, :].reshape(half * local, width)
        wide = latents.astype(jnp.float32)
        latent_norms = jnp.sum(wide * wide, axis=1, keepdims=True) * factor
        latent_norms = jnp.transpose(jnp.broadcast_to(latent_norms, (half * local, 128)))[:1, :]
        cross = lax.dot_general(
            noise, latents, (((1,), (1,)), ((), ())), preferred_element_type=jnp.float32
        )
        out_ref[...] = noise_norms + latent_norms - (2.0 * factor) * cross


def spread_kernel(parts_ref, out_ref):
    out_ref[...] = jnp.broadcast_to(jnp.sum(parts_ref[...], axis=0)[None], out_ref.shape)


def spread(parts, copies):
    return pl.pallas_call(
        spread_kernel,
        out_shape=jax.ShapeDtypeStruct((copies, *parts.shape[1:]), parts.dtype),
        in_specs=[VMEM],
        out_specs=VMEM,
        compiler_params=LIMIT,
    )(parts)


def exchange(blocks, axes):
    return lax.all_to_all(blocks, axes, 0, 0, tiled=True)


def coupling_kernel(core_ref, group_ref, own_ref, other_ref, clips_ref, moved_ref, row_ref, column_ref):
    scores = (own_ref, other_ref)
    sources, both, width = clips_ref.shape
    local = both // 2
    core = core_ref[0]
    total = sources * local
    log_mass = -math.log2(total)
    row = jnp.zeros((total, 1), jnp.float32)
    columns = [None] * CORES
    for step in range(ITERS):
        for k, score in enumerate(scores):
            value = row - score[...]
            top = jnp.max(value, axis=0, keepdims=True)
            mass = jnp.sum(jnp.exp2(value - top), axis=0, keepdims=True)
            columns[k] = log_mass - (top + jnp.log2(mass))
        values = [column - score[...] for column, score in zip(columns, scores, strict=True)]
        top = jnp.max(jnp.maximum(*values), axis=1, keepdims=True)
        mass = jnp.sum(sum(jnp.exp2(value - top) for value in values), axis=1, keepdims=True)
        row = log_mass - (top + jnp.log2(mass))
    noise = clips_ref[:, :local, :].reshape(total, width)
    back = BLUR * math.log(2.0)
    row_ref[...] = jnp.transpose(jnp.broadcast_to(row * back, (total, 128)))[:1, :]
    group = group_ref[0]
    half = total // CORES
    column = jnp.where(group * local // half == core, *columns) * back
    column = pltpu.roll(column, lax.rem(half - lax.rem(group * local, half), half), 1)
    column_ref[...] = column[:, :local]
    for k, (column, score) in enumerate(zip(columns, scores, strict=True)):
        place = core if k == 0 else 1 - core
        plan = jnp.exp2((row + column) - score[...])
        weights = (plan * (1.0 / jnp.sum(plan, axis=0, keepdims=True))).astype(jnp.bfloat16)
        moved = lax.dot_general(
            weights, noise, (((0,), (0,)), ((), ())), preferred_element_type=jnp.float32
        )
        moved_ref[place] = moved.astype(jnp.bfloat16)


def per_device(latents, noise):
    local, channels, width = latents.shape
    dp, seq, near = lax.axis_size(DP), lax.axis_size(SEQ), lax.axis_size(NEAR)
    total = local * dp
    half = total // CORES
    factor = math.log2(math.e) / (BLUR * math.sqrt(channels * width * seq))
    core = lax.axis_index("c").reshape(1).astype(jnp.int32)
    group = lax.axis_index(DP).reshape(1).astype(jnp.int32)
    swap = [(0, 1), (1, 0)]

    packed = pl.pallas_call(
        pack_kernel,
        out_shape=jax.ShapeDtypeStruct((channels, 2 * local, width), noise.dtype),
        in_specs=[HBM, HBM],
        out_specs=VMEM,
        scratch_shapes=[
            pltpu.VMEM((2, *noise.shape), noise.dtype),
            pltpu.SemaphoreType.DMA((2,)),
        ],
        compiler_params=LIMIT,
    )(*(pltpu.with_memory_space_constraint(given, pltpu.HBM) for given in (noise, latents)))
    packed, core, group = lax.optimization_barrier((packed, core, group))
    clips = exchange(packed, DP)

    block = jax.ShapeDtypeStruct((total, half), jnp.float32)
    send, keep = pl.pallas_call(
        functools.partial(pair_kernel, factor),
        out_shape=(block, block),
        in_specs=[SMEM, VMEM],
        out_specs=(VMEM, VMEM),
        compiler_params=LIMIT,
    )(core, clips)
    summed = keep + lax.ppermute(send, "c", swap)

    parts = exchange(summed.reshape(near, total // near, half), NEAR)
    parts = exchange(spread(parts, lax.axis_size("h")), "h")
    parts = exchange(spread(parts, lax.axis_size("q")), "q")
    own = exchange(spread(parts, near), NEAR).reshape(total, half)
    other = lax.ppermute(own, "c", swap)

    moved, row, column = pl.pallas_call(
        coupling_kernel,
        out_shape=(
            jax.ShapeDtypeStruct((CORES, half, width), jnp.bfloat16),
            jax.ShapeDtypeStruct((1, total), jnp.float32),
            jax.ShapeDtypeStruct((1, local), jnp.float32),
        ),
        in_specs=[SMEM, SMEM, VMEM, VMEM, VMEM],
        out_specs=(VMEM, VMEM, VMEM),
        compiler_params=LIMIT,
    )(core, group, own, other, clips)
    targets = exchange(moved.reshape(dp, local, width), DP).swapaxes(0, 1)
    return (targets, row.reshape(total), column.reshape(local))


def solution(mesh):
    fine = Mesh(mesh.devices.reshape(tuple(FINE.values())), tuple(FINE))
    in_specs = (P(DP, None, SEQ), P(DP, None, SEQ))
    out_specs = (P(DP, None, SEQ), P(), P(DP))
    return jax.shard_map(
        per_device, mesh=fine, in_specs=in_specs, out_specs=out_specs, check_vma=False
    )
```

```python
import functools
import math

import jax
import jax.numpy as jnp
from jax import lax
from jax.experimental import pallas as pl
from jax.experimental.pallas import tpu as pltpu
from jax.sharding import Mesh, PartitionSpec as P

ITERS = 4
BLUR = 0.5
FINE = {"z": 2, "q": 4, "p": 2, "h": 4, "x": 4, "c": 2}
DP = ("z", "q", "p")
SEQ = ("h", "x", "c")
NEAR = ("x", "z", "p")
ANY = pl.BlockSpec(memory_space=pl.ANY)
HBM = pl.BlockSpec(memory_space=pltpu.HBM)
VMEM = pl.BlockSpec(memory_space=pltpu.VMEM)
SMEM = pl.BlockSpec(memory_space=pltpu.SMEM)
LIMIT = pltpu.CompilerParams(vmem_limit_bytes=32 * 1024 * 1024)


def pack_kernel(noise_ref, latents_ref, out_ref, held, arrived):
    local = noise_ref.shape[0]
    copies = [
        pltpu.make_async_copy(given, held.at[k], arrived.at[k])
        for k, given in enumerate((noise_ref, latents_ref))
    ]
    for copy in copies:
        copy.start()
    for k, copy in enumerate(copies):
        copy.wait()
        out_ref[:, k * local : (k + 1) * local, :] = jnp.swapaxes(held[k], 0, 1)


def pair_kernel(factor, clips_ref, out_ref):
    sources, both, width = clips_ref.shape
    local = both // 2
    noise = clips_ref[:, :local, :].reshape(sources * local, width)
    latents = clips_ref[:, local:, :].reshape(sources * local, width)
    wide = noise.astype(jnp.float32)
    noise_norms = jnp.sum(wide * wide, axis=1, keepdims=True) * factor
    wide = latents.astype(jnp.float32)
    latent_norms = jnp.sum(wide * wide, axis=1, keepdims=True) * factor
    latent_norms = jnp.transpose(jnp.broadcast_to(latent_norms, (sources * local, 128)))[:1, :]
    cross = lax.dot_general(
        noise, latents, (((1,), (1,)), ((), ())), preferred_element_type=jnp.float32
    )
    out_ref[...] = noise_norms + latent_norms - (2.0 * factor) * cross


def spread_kernel(parts_ref, out_ref):
    out_ref[...] = jnp.broadcast_to(jnp.sum(parts_ref[...], axis=0)[None], out_ref.shape)


def spread(parts, copies):
    return pl.pallas_call(
        spread_kernel,
        out_shape=jax.ShapeDtypeStruct((copies, *parts.shape[1:]), parts.dtype),
        in_specs=[VMEM],
        out_specs=VMEM,
        compiler_params=LIMIT,
    )(parts)


def exchange(blocks, axes):
    return lax.all_to_all(blocks, axes, 0, 0, tiled=True)


def weigh(group, local, scores, row_ref, column_ref):
    total = scores.shape[0]
    log_mass = -math.log2(total)
    row = jnp.zeros((total, 1), jnp.float32)
    for step in range(ITERS):
        value = row - scores[...]
        top = jnp.max(value, axis=0, keepdims=True)
        mass = jnp.sum(jnp.exp2(value - top), axis=0, keepdims=True)
        column = log_mass - (top + jnp.log2(mass))
        value = column - scores[...]
        top = jnp.max(value, axis=1, keepdims=True)
        mass = jnp.sum(jnp.exp2(value - top), axis=1, keepdims=True)
        row = log_mass - (top + jnp.log2(mass))
    back = BLUR * math.log(2.0)
    row_ref[...] = jnp.transpose(jnp.broadcast_to(row * back, (total, 128)))[:1, :]
    placed = pltpu.roll(column * back, lax.rem(total - group * local, total), 1)
    column_ref[...] = placed[:, :local]
    plan = jnp.exp2((row + column) - scores[...])
    return (plan * (1.0 / jnp.sum(plan, axis=0, keepdims=True))).astype(jnp.bfloat16)


def far_kernel(group_ref, scores, clips_ref, moved_ref, row_ref, column_ref):
    sources, both, width = clips_ref.shape
    local = both // 2
    weights = weigh(group_ref[0], local, scores, row_ref, column_ref)
    noise = clips_ref[:, :local, :].reshape(sources * local, width)
    moved = lax.dot_general(
        weights, noise, (((0,), (0,)), ((), ())), preferred_element_type=jnp.float32
    )
    moved_ref[...] = moved.astype(jnp.bfloat16).reshape(moved_ref.shape)


def blank_kernel(out_ref):
    pass


def blank(shape, dtype):
    return pl.pallas_call(
        blank_kernel, out_shape=jax.ShapeDtypeStruct(shape, dtype), out_specs=ANY
    )()


def per_device(latents, noise):
    local, channels, width = latents.shape
    dp, seq, near = lax.axis_size(DP), lax.axis_size(SEQ), lax.axis_size(NEAR)
    total = local * dp
    factor = math.log2(math.e) / (BLUR * math.sqrt(channels * width * seq))
    group = lax.axis_index(DP).reshape(1).astype(jnp.int32)

    packed = pl.pallas_call(
        pack_kernel,
        out_shape=jax.ShapeDtypeStruct((channels, 2 * local, width), noise.dtype),
        in_specs=[HBM, HBM],
        out_specs=VMEM,
        scratch_shapes=[
            pltpu.VMEM((2, *noise.shape), noise.dtype),
            pltpu.SemaphoreType.DMA((2,)),
        ],
        compiler_params=LIMIT,
    )(*(pltpu.with_memory_space_constraint(given, pltpu.HBM) for given in (noise, latents)))
    packed, group = lax.optimization_barrier((packed, group))
    clips = exchange(packed, DP)

    terms = pl.pallas_call(
        functools.partial(pair_kernel, factor),
        out_shape=jax.ShapeDtypeStruct((total, total), jnp.float32),
        in_specs=[VMEM],
        out_specs=VMEM,
        compiler_params=LIMIT,
    )(clips)
    summed = terms + lax.ppermute(terms, "c", [(0, 1)])

    def reduce_cost(summed):
        parts = exchange(summed.reshape(near, total // near, total), NEAR)
        parts = exchange(spread(parts, lax.axis_size("h")), "h")
        parts = exchange(spread(parts, lax.axis_size("q")), "q")
        return exchange(spread(parts, near), NEAR).reshape(total, total)

    def move(cost, clips, group):
        moved, row, column = pl.pallas_call(
            far_kernel,
            out_shape=(jax.ShapeDtypeStruct((dp, local, width), noise.dtype), *ends),
            in_specs=[SMEM, VMEM, VMEM],
            out_specs=(VMEM, VMEM, VMEM),
            compiler_params=LIMIT,
        )(group, cost, clips)
        return exchange(moved, DP), row, column

    ends = (jax.ShapeDtypeStruct((1, total), jnp.float32), jax.ShapeDtypeStruct((1, local), jnp.float32))
    upper = lax.axis_index("c") == 1
    cost = lax.cond(upper, reduce_cost, lambda summed: blank((total, total), jnp.float32), summed)
    sent = lax.ppermute(cost, "c", [(1, 0)])
    done = lax.cond(
        upper,
        move,
        lambda cost, clips, group: (blank((dp, local, width), noise.dtype), *(blank(e.shape, e.dtype) for e in ends)),
        cost, clips, group,
    )
    targets, row, column = lax.cond(
        upper, lambda done, sent, clips, group: done, lambda done, sent, clips, group: move(sent, clips, group), done, sent, clips, group
    )
    return (targets.swapaxes(0, 1), row.reshape(total), column.reshape(local))


def solution(mesh):
    fine = Mesh(mesh.devices.reshape(tuple(FINE.values())), tuple(FINE))
    in_specs = (P(DP, None, SEQ), P(DP, None, SEQ))
    out_specs = (P(DP, None, SEQ), P(), P(DP))
    return jax.shard_map(
        per_device, mesh=fine, in_specs=in_specs, out_specs=out_specs, check_vma=False
    )
```

```python
import functools
import math

import jax
import jax.numpy as jnp
from jax import lax
from jax.experimental import pallas as pl
from jax.experimental.pallas import tpu as pltpu
from jax.sharding import Mesh, PartitionSpec as P

ITERS = 4
BLUR = 0.5
FINE = {"z": 2, "q": 4, "p": 2, "h": 4, "x": 4, "c": 2}
DP = ("z", "q", "p")
SEQ = ("h", "x", "c")
NEAR = ("x", "z", "p")
ANY = pl.BlockSpec(memory_space=pl.ANY)
HBM = pl.BlockSpec(memory_space=pltpu.HBM)
VMEM = pl.BlockSpec(memory_space=pltpu.VMEM)
SMEM = pl.BlockSpec(memory_space=pltpu.SMEM)
LIMIT = pltpu.CompilerParams(vmem_limit_bytes=32 * 1024 * 1024)


def pack_kernel(noise_ref, latents_ref, *rest):
    *out_refs, held, arrived = rest
    local = noise_ref.shape[0]
    copies = [
        pltpu.make_async_copy(given, held.at[k], arrived.at[k])
        for k, given in enumerate((noise_ref, latents_ref))
    ]
    for copy in copies:
        copy.start()
    for k, copy in enumerate(copies):
        copy.wait()
        turned = jnp.swapaxes(held[k], 0, 1)
        first = 0
        for out_ref in out_refs:
            last = first + out_ref.shape[1]
            low, high = max(first, k * local), min(last, (k + 1) * local)
            if low < high:
                out_ref[:, low - first : high - first, :] = turned[:, low - k * local : high - k * local, :]
            first = last


def pack(noise, latents, runs):
    local, channels, width = noise.shape
    return pl.pallas_call(
        pack_kernel,
        out_shape=tuple(jax.ShapeDtypeStruct((channels, rows, width), noise.dtype) for rows in runs),
        in_specs=[HBM, HBM],
        out_specs=(VMEM,) * len(runs),
        scratch_shapes=[
            pltpu.VMEM((2, *noise.shape), noise.dtype),
            pltpu.SemaphoreType.DMA((2,)),
        ],
        compiler_params=LIMIT,
    )(*(pltpu.with_memory_space_constraint(given, pltpu.HBM) for given in (noise, latents)))


def noise_of(local, head_ref, rest_ref):
    sources, head, width = head_ref.shape
    noise = jnp.concatenate([head_ref[...], rest_ref[:, : local - head, :]], axis=1)
    return noise.reshape(sources * local, width)


def pair_kernel(factor, head_ref, rest_ref, out_ref, *tail_refs):
    sources, head, width = head_ref.shape
    local = (head + rest_ref.shape[1]) // 2
    total = sources * local
    noise = noise_of(local, head_ref, rest_ref)
    latents = rest_ref[:, local - head :, :].reshape(total, width)
    wide = noise.astype(jnp.float32)
    noise_norms = jnp.sum(wide * wide, axis=1, keepdims=True) * factor
    wide = latents.astype(jnp.float32)
    latent_norms = jnp.sum(wide * wide, axis=1, keepdims=True) * factor
    latent_norms = jnp.transpose(jnp.broadcast_to(latent_norms, (total, 128)))[:1, :]
    cross = lax.dot_general(
        noise, latents, (((1,), (1,)), ((), ())), preferred_element_type=jnp.float32
    )
    out_ref[...] = noise_norms + latent_norms - (2.0 * factor) * cross
    for tail_ref in tail_refs:
        tail_ref[...] = rest_ref[:, : local - head, :]


def spread_kernel(parts_ref, out_ref):
    out_ref[...] = jnp.broadcast_to(jnp.sum(parts_ref[...], axis=0)[None], out_ref.shape)


def spread(parts, copies):
    return pl.pallas_call(
        spread_kernel,
        out_shape=jax.ShapeDtypeStruct((copies, *parts.shape[1:]), parts.dtype),
        in_specs=[VMEM],
        out_specs=VMEM,
        compiler_params=LIMIT,
    )(parts)


def exchange(blocks, axes):
    return lax.all_to_all(blocks, axes, 0, 0, tiled=True)


def weigh(group, local, scores, row_ref, column_ref):
    total = scores.shape[0]
    log_mass = -math.log2(total)
    row = jnp.zeros((total, 1), jnp.float32)
    for step in range(ITERS):
        value = row - scores[...]
        top = jnp.max(value, axis=0, keepdims=True)
        mass = jnp.sum(jnp.exp2(value - top), axis=0, keepdims=True)
        column = log_mass - (top + jnp.log2(mass))
        value = column - scores[...]
        top = jnp.max(value, axis=1, keepdims=True)
        mass = jnp.sum(jnp.exp2(value - top), axis=1, keepdims=True)
        row = log_mass - (top + jnp.log2(mass))
    back = BLUR * math.log(2.0)
    row_ref[...] = jnp.transpose(jnp.broadcast_to(row * back, (total, 128)))[:1, :]
    placed = pltpu.roll(column * back, lax.rem(total - group * local, total), 1)
    column_ref[...] = placed[:, :local]
    plan = jnp.exp2((row + column) - scores[...])
    return (plan * (1.0 / jnp.sum(plan, axis=0, keepdims=True))).astype(jnp.bfloat16)


def coupling_kernel(group_ref, scores, head_ref, rest_ref, moved_ref, row_ref, column_ref):
    local = column_ref.shape[1]
    noise = noise_of(local, head_ref, rest_ref)
    weights = weigh(group_ref[0], local, scores, row_ref, column_ref)
    moved = lax.dot_general(
        weights, noise, (((0,), (0,)), ((), ())), preferred_element_type=jnp.float32
    )
    moved_ref[...] = moved.astype(jnp.bfloat16).reshape(moved_ref.shape)


def blank_kernel(out_ref):
    pass


def blank(shape, dtype):
    return pl.pallas_call(
        blank_kernel, out_shape=jax.ShapeDtypeStruct(shape, dtype), out_specs=ANY
    )()


def per_device(latents, noise):
    local, channels, width = latents.shape
    dp, seq, near = lax.axis_size(DP), lax.axis_size(SEQ), lax.axis_size(NEAR)
    total = local * dp
    factor = math.log2(math.e) / (BLUR * math.sqrt(channels * width * seq))
    group = lax.axis_index(DP).reshape(1).astype(jnp.int32)

    head = local // 2
    upper = lax.axis_index("c") == 1

    square = (total, total)

    tail = (dp, local - head, width)

    def pair_terms(clips, tails=0):
        return pl.pallas_call(
            functools.partial(pair_kernel, factor),
            out_shape=(jax.ShapeDtypeStruct(square, jnp.float32),)
            + (jax.ShapeDtypeStruct(tail, noise.dtype),) * tails,
            in_specs=[VMEM, VMEM],
            out_specs=(VMEM,) * (1 + tails),
            compiler_params=LIMIT,
        )(*clips)

    def start_upper(noise, latents):
        first, second = pack(noise, latents, (head, 2 * local - head))
        first, second, unused = lax.optimization_barrier((first, second, blank(square, jnp.float32)))
        first, second = lax.optimization_barrier((exchange(first, DP), second))
        return first, second, unused

    def start_lower(noise, latents):
        (packed,) = pack(noise, latents, (2 * local,))
        clips = exchange(packed, DP)
        clips = clips[:, :head], clips[:, head:]
        return *clips, *pair_terms(clips)

    def finish_upper(first, second):
        return pair_terms((first, exchange(second, DP)), tails=1)

    def finish_lower(first, second):
        return blank(square, jnp.float32), blank(tail, noise.dtype)

    first, second, terms = lax.cond(upper, start_upper, start_lower, noise, latents)
    received = lax.ppermute(terms, "c", [(0, 1)])
    upper_terms, upper_noise = lax.cond(upper, finish_upper, finish_lower, first, second)

    def reduce_cost(terms, received):
        summed = terms + received
        parts = exchange(summed.reshape(near, total // near, total), NEAR)
        parts = exchange(spread(parts, lax.axis_size("h")), "h")
        parts = exchange(spread(parts, lax.axis_size("q")), "q")
        return exchange(spread(parts, near), NEAR).reshape(total, total)

    def move(cost, clips, group):
        moved, row, column = pl.pallas_call(
            coupling_kernel,
            out_shape=(jax.ShapeDtypeStruct((dp, local, width), noise.dtype), *ends),
            in_specs=[SMEM, VMEM, VMEM, VMEM],
            out_specs=(VMEM, VMEM, VMEM),
            compiler_params=LIMIT,
        )(group, cost, *clips)
        return exchange(moved, DP), row, column

    ends = (jax.ShapeDtypeStruct((1, total), jnp.float32), jax.ShapeDtypeStruct((1, local), jnp.float32))
    cost = lax.cond(
        upper, reduce_cost, lambda terms, received: blank(square, jnp.float32), upper_terms, received
    )
    sent = lax.ppermute(cost, "c", [(1, 0)])
    done = lax.cond(
        upper,
        move,
        lambda cost, clips, group: (blank((dp, local, width), noise.dtype), *(blank(e.shape, e.dtype) for e in ends)),
        cost,
        (first, upper_noise),
        group,
    )
    targets, row, column = lax.cond(
        upper,
        lambda done, sent, clips, group: done,
        lambda done, sent, clips, group: move(sent, clips, group),
        done,
        sent,
        (first, second),
        group,
    )
    return (targets.swapaxes(0, 1), row.reshape(total), column.reshape(local))


def solution(mesh):
    fine = Mesh(mesh.devices.reshape(tuple(FINE.values())), tuple(FINE))
    in_specs = (P(DP, None, SEQ), P(DP, None, SEQ))
    out_specs = (P(DP, None, SEQ), P(), P(DP))
    return jax.shard_map(
        per_device, mesh=fine, in_specs=in_specs, out_specs=out_specs, check_vma=False
    )
```

```python
import functools
import math

import jax
import jax.numpy as jnp
from jax import lax
from jax.experimental import pallas as pl
from jax.experimental.pallas import tpu as pltpu
from jax.sharding import Mesh, PartitionSpec as P

ITERS = 4
PARTS = 2
BLUR = 0.5
FINE = {"z": 2, "q": 4, "p": 2, "h": 4, "x": 4, "c": 2}
DP = ("z", "q", "p")
SEQ = ("h", "x", "c")
NEAR = ("x", "z", "p")
ANY = pl.BlockSpec(memory_space=pl.ANY)
HBM = pl.BlockSpec(memory_space=pltpu.HBM)
VMEM = pl.BlockSpec(memory_space=pltpu.VMEM)
SMEM = pl.BlockSpec(memory_space=pltpu.SMEM)
LIMIT = pltpu.CompilerParams(vmem_limit_bytes=32 * 1024 * 1024)


def pack_kernel(noise_ref, latents_ref, *rest):
    *out_refs, held, arrived = rest
    local, _, width = noise_ref.shape
    width //= PARTS
    copies = [
        pltpu.make_async_copy(given, held.at[k], arrived.at[k])
        for k, given in enumerate((noise_ref, latents_ref))
    ]
    for copy in copies:
        copy.start()
    for k, copy in enumerate(copies):
        copy.wait()
        turned = jnp.swapaxes(held[k], 0, 1)
        for part in range(PARTS):
            start = (part * 2 + k) * local
            piece = turned[:, :, part * width : (part + 1) * width]
            first = 0
            for out_ref in out_refs:
                last = first + out_ref.shape[1]
                low, high = max(first, start), min(last, start + local)
                if low < high:
                    out_ref[:, low - first : high - first, :] = piece[:, low - start : high - start, :]
                first = last


def pack(noise, latents, runs):
    local, channels, width = noise.shape
    return pl.pallas_call(
        pack_kernel,
        out_shape=tuple(jax.ShapeDtypeStruct((channels, rows, width // PARTS), noise.dtype) for rows in runs),
        in_specs=[HBM, HBM],
        out_specs=(VMEM,) * len(runs),
        scratch_shapes=[
            pltpu.VMEM((2, *noise.shape), noise.dtype),
            pltpu.SemaphoreType.DMA((2,)),
        ],
        compiler_params=LIMIT,
    )(*(pltpu.with_memory_space_constraint(given, pltpu.HBM) for given in (noise, latents)))


def noise_of(head_ref, rest_ref, local, skipped):
    sources, head, width = head_ref.shape
    tail = local - head
    first = jnp.concatenate([head_ref[...], rest_ref[:, :tail, :]], axis=1)
    second = rest_ref[:, tail + skipped : tail + skipped + local, :]
    return [noise.reshape(sources * local, width) for noise in (first, second)]


def pair_kernel(factor, head_ref, rest_ref, out_ref, *tail_refs):
    sources, head, width = head_ref.shape
    local = (head + rest_ref.shape[1]) // (2 * PARTS)
    total = sources * local
    tail = local - head
    noises = noise_of(head_ref, rest_ref, local, local)
    terms = 0.0
    for part, noise in enumerate(noises):
        first = tail + 2 * part * local
        latents = rest_ref[:, first : first + local, :].reshape(total, width)
        wide = noise.astype(jnp.float32)
        noise_norms = jnp.sum(wide * wide, axis=1, keepdims=True) * factor
        wide = latents.astype(jnp.float32)
        latent_norms = jnp.sum(wide * wide, axis=1, keepdims=True) * factor
        latent_norms = jnp.transpose(jnp.broadcast_to(latent_norms, (total, 128)))[:1, :]
        cross = lax.dot_general(
            noise, latents, (((1,), (1,)), ((), ())), preferred_element_type=jnp.float32
        )
        terms += noise_norms + latent_norms - (2.0 * factor) * cross
    out_ref[...] = terms
    for tail_ref in tail_refs:
        tail_ref[:, :tail, :] = rest_ref[:, :tail, :]
        tail_ref[:, tail:, :] = rest_ref[:, tail + local : tail + 2 * local, :]


def spread_kernel(parts_ref, out_ref):
    out_ref[...] = jnp.broadcast_to(jnp.sum(parts_ref[...], axis=0)[None], out_ref.shape)


def spread(parts, copies):
    return pl.pallas_call(
        spread_kernel,
        out_shape=jax.ShapeDtypeStruct((copies, *parts.shape[1:]), parts.dtype),
        in_specs=[VMEM],
        out_specs=VMEM,
        compiler_params=LIMIT,
    )(parts)


def exchange(blocks, axes):
    return lax.all_to_all(blocks, axes, 0, 0, tiled=True)


def weigh(group, local, scores, row_ref, column_ref):
    total = scores.shape[0]
    log_mass = -math.log2(total)
    row = jnp.zeros((total, 1), jnp.float32)
    for step in range(ITERS):
        value = row - scores[...]
        top = jnp.max(value, axis=0, keepdims=True)
        mass = jnp.sum(jnp.exp2(value - top), axis=0, keepdims=True)
        column = log_mass - (top + jnp.log2(mass))
        value = column - scores[...]
        top = jnp.max(value, axis=1, keepdims=True)
        mass = jnp.sum(jnp.exp2(value - top), axis=1, keepdims=True)
        row = log_mass - (top + jnp.log2(mass))
    back = BLUR * math.log(2.0)
    row_ref[...] = jnp.transpose(jnp.broadcast_to(row * back, (total, 128)))[:1, :]
    placed = pltpu.roll(column * back, lax.rem(total - group * local, total), 1)
    column_ref[...] = placed[:, :local]
    plan = jnp.exp2((row + column) - scores[...])
    return (plan * (1.0 / jnp.sum(plan, axis=0, keepdims=True))).astype(jnp.bfloat16)


def coupling_kernel(skipped, group_ref, scores, head_ref, rest_ref, moved_ref, row_ref, column_ref):
    local = column_ref.shape[1]
    width = head_ref.shape[2]
    weights = weigh(group_ref[0], local, scores, row_ref, column_ref)
    for part, noise in enumerate(noise_of(head_ref, rest_ref, local, skipped)):
        moved = lax.dot_general(
            weights, noise, (((0,), (0,)), ((), ())), preferred_element_type=jnp.float32
        )
        moved = moved.astype(jnp.bfloat16).reshape(-1, local, width)
        moved_ref[:, :, part * width : (part + 1) * width] = moved


def blank_kernel(out_ref):
    pass


def blank(shape, dtype):
    return pl.pallas_call(
        blank_kernel, out_shape=jax.ShapeDtypeStruct(shape, dtype), out_specs=ANY
    )()


def per_device(latents, noise):
    local, channels, width = latents.shape
    dp, seq, near = lax.axis_size(DP), lax.axis_size(SEQ), lax.axis_size(NEAR)
    total = local * dp
    factor = math.log2(math.e) / (BLUR * math.sqrt(channels * width * seq))
    group = lax.axis_index(DP).reshape(1).astype(jnp.int32)

    head = local // 2
    upper = lax.axis_index("c") == 1

    square = (total, total)

    tail = (dp, PARTS * local - head, width // PARTS)

    def pair_terms(clips, tails=0):
        return pl.pallas_call(
            functools.partial(pair_kernel, factor),
            out_shape=(jax.ShapeDtypeStruct(square, jnp.float32),)
            + (jax.ShapeDtypeStruct(tail, noise.dtype),) * tails,
            in_specs=[VMEM, VMEM],
            out_specs=(VMEM,) * (1 + tails),
            compiler_params=LIMIT,
        )(*clips)

    def start_upper(noise, latents):
        first, second = pack(noise, latents, (head, 2 * PARTS * local - head))
        first, second, unused = lax.optimization_barrier((first, second, blank(square, jnp.float32)))
        first, second = lax.optimization_barrier((exchange(first, DP), second))
        return first, second, unused

    def start_lower(noise, latents):
        (packed,) = pack(noise, latents, (2 * PARTS * local,))
        clips = exchange(packed, DP)
        clips = clips[:, :head], clips[:, head:]
        return *clips, *pair_terms(clips)

    def finish_upper(first, second):
        return pair_terms((first, exchange(second, DP)), tails=1)

    def finish_lower(first, second):
        return blank(square, jnp.float32), blank(tail, noise.dtype)

    first, second, terms = lax.cond(upper, start_upper, start_lower, noise, latents)
    received = lax.ppermute(terms, "c", [(0, 1)])
    upper_terms, upper_noise = lax.cond(upper, finish_upper, finish_lower, first, second)

    def reduce_cost(terms, received):
        summed = terms + received
        parts = exchange(summed.reshape(near, total // near, total), NEAR)
        parts = exchange(spread(parts, lax.axis_size("h")), "h")
        parts = exchange(spread(parts, lax.axis_size("q")), "q")
        return exchange(spread(parts, near), NEAR).reshape(total, total)

    def move(skipped, cost, clips, group):
        moved, row, column = pl.pallas_call(
            functools.partial(coupling_kernel, skipped),
            out_shape=(jax.ShapeDtypeStruct((dp, local, width), noise.dtype), *ends),
            in_specs=[SMEM, VMEM, VMEM, VMEM],
            out_specs=(VMEM, VMEM, VMEM),
            compiler_params=LIMIT,
        )(group, cost, *clips)
        return exchange(moved, DP), row, column

    ends = (jax.ShapeDtypeStruct((1, total), jnp.float32), jax.ShapeDtypeStruct((1, local), jnp.float32))
    cost = lax.cond(
        upper, reduce_cost, lambda terms, received: blank(square, jnp.float32), upper_terms, received
    )
    sent = lax.ppermute(cost, "c", [(1, 0)])
    done = lax.cond(
        upper,
        functools.partial(move, 0),
        lambda cost, clips, group: (blank((dp, local, width), noise.dtype), *(blank(e.shape, e.dtype) for e in ends)),
        cost,
        (first, upper_noise),
        group,
    )
    targets, row, column = lax.cond(
        upper,
        lambda done, sent, clips, group: done,
        lambda done, sent, clips, group: move(local, sent, clips, group),
        done,
        sent,
        (first, second),
        group,
    )
    return (targets.swapaxes(0, 1), row.reshape(total), column.reshape(local))


def solution(mesh):
    fine = Mesh(mesh.devices.reshape(tuple(FINE.values())), tuple(FINE))
    in_specs = (P(DP, None, SEQ), P(DP, None, SEQ))
    out_specs = (P(DP, None, SEQ), P(), P(DP))
    return jax.shard_map(
        per_device, mesh=fine, in_specs=in_specs, out_specs=out_specs, check_vma=False
    )
```

```python
import functools
import math

import jax
import jax.numpy as jnp
from jax import lax
from jax.experimental import pallas as pl
from jax.experimental.pallas import tpu as pltpu
from jax.sharding import Mesh, PartitionSpec as P

ITERS = 4
PARTS = 4
BLUR = 0.5
FINE = {"z": 2, "q": 4, "p": 2, "h": 4, "x": 4, "c": 2}
DP = ("z", "q", "p")
SEQ = ("h", "x", "c")
NEAR = ("x", "z", "p")
ANY = pl.BlockSpec(memory_space=pl.ANY)
HBM = pl.BlockSpec(memory_space=pltpu.HBM)
VMEM = pl.BlockSpec(memory_space=pltpu.VMEM)
SMEM = pl.BlockSpec(memory_space=pltpu.SMEM)
LIMIT = pltpu.CompilerParams(vmem_limit_bytes=32 * 1024 * 1024)


def pack_kernel(noise_ref, latents_ref, *rest):
    *out_refs, held, arrived = rest
    local, _, width = noise_ref.shape
    width //= PARTS
    copies = [
        pltpu.make_async_copy(given, held.at[k], arrived.at[k])
        for k, given in enumerate((noise_ref, latents_ref))
    ]
    for copy in copies:
        copy.start()
    for k, copy in enumerate(copies):
        copy.wait()
        turned = jnp.swapaxes(held[k], 0, 1)
        for part in range(PARTS):
            start = (part * 2 + k) * local
            piece = turned[:, :, part * width : (part + 1) * width]
            first = 0
            for out_ref in out_refs:
                last = first + out_ref.shape[1]
                low, high = max(first, start), min(last, start + local)
                if low < high:
                    out_ref[:, low - first : high - first, :] = piece[:, low - start : high - start, :]
                first = last


def pack(noise, latents, runs):
    local, channels, width = noise.shape
    return pl.pallas_call(
        pack_kernel,
        out_shape=tuple(jax.ShapeDtypeStruct((channels, rows, width // PARTS), noise.dtype) for rows in runs),
        in_specs=[HBM, HBM],
        out_specs=(VMEM,) * len(runs),
        scratch_shapes=[
            pltpu.VMEM((2, *noise.shape), noise.dtype),
            pltpu.SemaphoreType.DMA((2,)),
        ],
        compiler_params=LIMIT,
    )(*(pltpu.with_memory_space_constraint(given, pltpu.HBM) for given in (noise, latents)))


def noise_of(head_ref, rest_ref, local, skipped):
    sources, head, width = head_ref.shape
    tail = local - head
    parts = [jnp.concatenate([head_ref[...], rest_ref[:, :tail, :]], axis=1)]
    for part in range(1, PARTS):
        first = tail + skipped + (part - 1) * (local + skipped)
        parts.append(rest_ref[:, first : first + local, :])
    return [part.reshape(sources * local, width) for part in parts]


def square_sums(parts):
    total = 0.0
    for part in parts:
        wide = part.astype(jnp.float32)
        total += wide * wide
    return jnp.sum(total, axis=1, keepdims=True)


def pair_kernel(factor, head_ref, rest_ref, out_ref, *tail_refs):
    sources, head, width = head_ref.shape
    local = (head + rest_ref.shape[1]) // (2 * PARTS)
    total = sources * local
    tail = local - head
    noises = noise_of(head_ref, rest_ref, local, local)
    latents = [
        rest_ref[:, first : first + local, :].reshape(total, width)
        for first in range(tail, rest_ref.shape[1], 2 * local)
    ]
    noise_norms = square_sums(noises) * factor
    latent_norms = square_sums(latents) * factor
    latent_norms = jnp.transpose(jnp.broadcast_to(latent_norms, (total, 128)))[:1, :]
    cross = lax.dot_general(
        jnp.concatenate(noises, axis=1),
        jnp.concatenate(latents, axis=1),
        (((1,), (1,)), ((), ())),
        preferred_element_type=jnp.float32,
    )
    out_ref[...] = noise_norms + latent_norms - (2.0 * factor) * cross
    for tail_ref in tail_refs:
        tail_ref[:, :tail, :] = rest_ref[:, :tail, :]
        for part in range(1, PARTS):
            first = tail + local + (part - 1) * 2 * local
            to = tail + (part - 1) * local
            tail_ref[:, to : to + local, :] = rest_ref[:, first : first + local, :]


def spread_kernel(parts_ref, out_ref):
    out_ref[...] = jnp.broadcast_to(jnp.sum(parts_ref[...], axis=0)[None], out_ref.shape)


def spread(parts, copies):
    return pl.pallas_call(
        spread_kernel,
        out_shape=jax.ShapeDtypeStruct((copies, *parts.shape[1:]), parts.dtype),
        in_specs=[VMEM],
        out_specs=VMEM,
        compiler_params=LIMIT,
    )(parts)


def exchange(blocks, axes):
    return lax.all_to_all(blocks, axes, 0, 0, tiled=True)


def weigh(group, local, scores, row_ref, column_ref):
    total = scores.shape[0]
    log_mass = -math.log2(total)
    row = jnp.zeros((total, 1), jnp.float32)
    for step in range(ITERS):
        value = row - scores[...]
        top = jnp.max(value, axis=0, keepdims=True)
        mass = jnp.sum(jnp.exp2(value - top), axis=0, keepdims=True)
        column = log_mass - (top + jnp.log2(mass))
        value = column - scores[...]
        top = jnp.max(value, axis=1, keepdims=True)
        mass = jnp.sum(jnp.exp2(value - top), axis=1, keepdims=True)
        row = log_mass - (top + jnp.log2(mass))
    back = BLUR * math.log(2.0)
    row_ref[...] = jnp.transpose(jnp.broadcast_to(row * back, (total, 128)))[:1, :]
    placed = pltpu.roll(column * back, lax.rem(total - group * local, total), 1)
    column_ref[...] = placed[:, :local]
    plan = jnp.exp2((row + column) - scores[...])
    return (plan * (1.0 / jnp.sum(plan, axis=0, keepdims=True))).astype(jnp.bfloat16)


def coupling_kernel(skipped, group_ref, scores, head_ref, rest_ref, moved_ref, row_ref, column_ref):
    local = column_ref.shape[1]
    weights = weigh(group_ref[0], local, scores, row_ref, column_ref)
    noise = jnp.concatenate(noise_of(head_ref, rest_ref, local, skipped), axis=1)
    moved = lax.dot_general(
        weights, noise, (((0,), (0,)), ((), ())), preferred_element_type=jnp.float32
    )
    moved_ref[...] = moved.astype(jnp.bfloat16).reshape(moved_ref.shape)


def blank_kernel(out_ref):
    pass


def blank(shape, dtype):
    return pl.pallas_call(
        blank_kernel, out_shape=jax.ShapeDtypeStruct(shape, dtype), out_specs=ANY
    )()


def per_device(latents, noise):
    local, channels, width = latents.shape
    dp, seq, near = lax.axis_size(DP), lax.axis_size(SEQ), lax.axis_size(NEAR)
    total = local * dp
    factor = math.log2(math.e) / (BLUR * math.sqrt(channels * width * seq))
    group = lax.axis_index(DP).reshape(1).astype(jnp.int32)

    head = local // 2
    upper = lax.axis_index("c") == 1

    square = (total, total)

    tail = (dp, PARTS * local - head, width // PARTS)

    def pair_terms(clips, tails=0):
        return pl.pallas_call(
            functools.partial(pair_kernel, factor),
            out_shape=(jax.ShapeDtypeStruct(square, jnp.float32),)
            + (jax.ShapeDtypeStruct(tail, noise.dtype),) * tails,
            in_specs=[VMEM, VMEM],
            out_specs=(VMEM,) * (1 + tails),
            compiler_params=LIMIT,
        )(*clips)

    def start_upper(noise, latents):
        first, second = pack(noise, latents, (head, 2 * PARTS * local - head))
        first, second, unused = lax.optimization_barrier((first, second, blank(square, jnp.float32)))
        first, second = lax.optimization_barrier((exchange(first, DP), second))
        return first, second, unused

    def start_lower(noise, latents):
        (packed,) = pack(noise, latents, (2 * PARTS * local,))
        clips = exchange(packed, DP)
        clips = clips[:, :head], clips[:, head:]
        return *clips, *pair_terms(clips)

    def finish_upper(first, second):
        return pair_terms((first, exchange(second, DP)), tails=1)

    def finish_lower(first, second):
        return blank(square, jnp.float32), blank(tail, noise.dtype)

    first, second, terms = lax.cond(upper, start_upper, start_lower, noise, latents)
    received = lax.ppermute(terms, "c", [(0, 1)])
    upper_terms, upper_noise = lax.cond(upper, finish_upper, finish_lower, first, second)

    def reduce_cost(terms, received):
        summed = terms + received
        parts = exchange(summed.reshape(near, total // near, total), NEAR)
        parts = exchange(spread(parts, lax.axis_size("h")), "h")
        parts = exchange(spread(parts, lax.axis_size("q")), "q")
        return exchange(spread(parts, near), NEAR).reshape(total, total)

    def move(skipped, cost, clips, group):
        moved, row, column = pl.pallas_call(
            functools.partial(coupling_kernel, skipped),
            out_shape=(jax.ShapeDtypeStruct((dp, local, width), noise.dtype), *ends),
            in_specs=[SMEM, VMEM, VMEM, VMEM],
            out_specs=(VMEM, VMEM, VMEM),
            compiler_params=LIMIT,
        )(group, cost, *clips)
        return exchange(moved, DP), row, column

    ends = (jax.ShapeDtypeStruct((1, total), jnp.float32), jax.ShapeDtypeStruct((1, local), jnp.float32))
    cost = lax.cond(
        upper, reduce_cost, lambda terms, received: blank(square, jnp.float32), upper_terms, received
    )
    sent = lax.ppermute(cost, "c", [(1, 0)])
    done = lax.cond(
        upper,
        functools.partial(move, 0),
        lambda cost, clips, group: (blank((dp, local, width), noise.dtype), *(blank(e.shape, e.dtype) for e in ends)),
        cost,
        (first, upper_noise),
        group,
    )
    targets, row, column = lax.cond(
        upper,
        lambda done, sent, clips, group: done,
        lambda done, sent, clips, group: move(local, sent, clips, group),
        done,
        sent,
        (first, second),
        group,
    )
    return (targets.swapaxes(0, 1), row.reshape(total), column.reshape(local))


def solution(mesh):
    fine = Mesh(mesh.devices.reshape(tuple(FINE.values())), tuple(FINE))
    in_specs = (P(DP, None, SEQ), P(DP, None, SEQ))
    out_specs = (P(DP, None, SEQ), P(), P(DP))
    return jax.shard_map(
        per_device, mesh=fine, in_specs=in_specs, out_specs=out_specs, check_vma=False
    )
```

```python
import functools
import math

import jax
import jax.numpy as jnp
from jax import lax
from jax.experimental import pallas as pl
from jax.experimental.pallas import tpu as pltpu
from jax.sharding import Mesh, PartitionSpec as P

ITERS = 4
PARTS = 2
BLUR = 0.5
FINE = {"z": 2, "q": 4, "p": 2, "h": 4, "x": 4, "c": 2}
DP = ("z", "q", "p")
SEQ = ("h", "x", "c")
NEAR = ("x", "z", "p")
ANY = pl.BlockSpec(memory_space=pl.ANY)
HBM = pl.BlockSpec(memory_space=pltpu.HBM)
VMEM = pl.BlockSpec(memory_space=pltpu.VMEM)
SMEM = pl.BlockSpec(memory_space=pltpu.SMEM)
LIMIT = pltpu.CompilerParams(vmem_limit_bytes=32 * 1024 * 1024)


def pack_kernel(noise_ref, latents_ref, *rest):
    *out_refs, held, arrived = rest
    local, _, width = noise_ref.shape
    width //= PARTS
    copies = [
        pltpu.make_async_copy(given, held.at[k], arrived.at[k])
        for k, given in enumerate((noise_ref, latents_ref))
    ]
    for copy in copies:
        copy.start()
    for k, copy in enumerate(copies):
        copy.wait()
        turned = jnp.swapaxes(held[k], 0, 1)
        for part in range(PARTS):
            start = (part * 2 + k) * local
            piece = turned[:, :, part * width : (part + 1) * width]
            first = 0
            for out_ref in out_refs:
                last = first + out_ref.shape[1]
                low, high = max(first, start), min(last, start + local)
                if low < high:
                    out_ref[:, low - first : high - first, :] = piece[:, low - start : high - start, :]
                first = last


def pack(noise, latents, runs):
    local, channels, width = noise.shape
    return pl.pallas_call(
        pack_kernel,
        out_shape=tuple(jax.ShapeDtypeStruct((channels, rows, width // PARTS), noise.dtype) for rows in runs),
        in_specs=[HBM, HBM],
        out_specs=(VMEM,) * len(runs),
        scratch_shapes=[
            pltpu.VMEM((2, *noise.shape), noise.dtype),
            pltpu.SemaphoreType.DMA((2,)),
        ],
        compiler_params=LIMIT,
    )(*(pltpu.with_memory_space_constraint(given, pltpu.HBM) for given in (noise, latents)))


def noise_of(head_ref, rest_ref, local, skipped):
    sources, head, width = head_ref.shape
    tail = local - head
    parts = [jnp.concatenate([head_ref[...], rest_ref[:, :tail, :]], axis=1)]
    for part in range(1, PARTS):
        first = tail + skipped + (part - 1) * (local + skipped)
        parts.append(rest_ref[:, first : first + local, :])
    return [part.reshape(sources * local, width) for part in parts]


def square_sums(parts):
    total = 0.0
    for part in parts:
        wide = part.astype(jnp.float32)
        total += wide * wide
    return jnp.sum(total, axis=1, keepdims=True)


def pair_kernel(factor, head_ref, rest_ref, out_ref, *tail_refs):
    sources, head, width = head_ref.shape
    local = (head + rest_ref.shape[1]) // (2 * PARTS)
    total = sources * local
    tail = local - head
    noises = noise_of(head_ref, rest_ref, local, local)
    latents = [
        rest_ref[:, first : first + local, :].reshape(total, width)
        for first in range(tail, rest_ref.shape[1], 2 * local)
    ]
    noise_norms = square_sums(noises) * factor
    latent_norms = square_sums(latents) * factor
    latent_norms = jnp.transpose(jnp.broadcast_to(latent_norms, (total, 128)))[:1, :]
    cross = lax.dot_general(
        jnp.concatenate(noises, axis=1),
        jnp.concatenate(latents, axis=1),
        (((1,), (1,)), ((), ())),
        preferred_element_type=jnp.float32,
    )
    out_ref[...] = noise_norms + latent_norms - (2.0 * factor) * cross
    for tail_ref in tail_refs:
        tail_ref[:, :tail, :] = rest_ref[:, :tail, :]
        for part in range(1, PARTS):
            first = tail + local + (part - 1) * 2 * local
            to = tail + (part - 1) * local
            tail_ref[:, to : to + local, :] = rest_ref[:, first : first + local, :]


def spread_kernel(parts_ref, out_ref):
    out_ref[...] = jnp.broadcast_to(jnp.sum(parts_ref[...], axis=0)[None], out_ref.shape)


def spread(parts, copies):
    return pl.pallas_call(
        spread_kernel,
        out_shape=jax.ShapeDtypeStruct((copies, *parts.shape[1:]), parts.dtype),
        in_specs=[VMEM],
        out_specs=VMEM,
        compiler_params=LIMIT,
    )(parts)


def exchange(blocks, axes):
    return lax.all_to_all(blocks, axes, 0, 0, tiled=True)


def weigh(group, local, scores, row_ref, column_ref):
    total = scores.shape[0]
    log_mass = -math.log2(total)
    row = jnp.zeros((total, 1), jnp.float32)
    for step in range(ITERS):
        value = row - scores[...]
        top = jnp.max(value, axis=0, keepdims=True)
        mass = jnp.sum(jnp.exp2(value - top), axis=0, keepdims=True)
        column = log_mass - (top + jnp.log2(mass))
        value = column - scores[...]
        top = jnp.max(value, axis=1, keepdims=True)
        mass = jnp.sum(jnp.exp2(value - top), axis=1, keepdims=True)
        row = log_mass - (top + jnp.log2(mass))
    back = BLUR * math.log(2.0)
    row_ref[...] = jnp.transpose(jnp.broadcast_to(row * back, (total, 128)))[:1, :]
    placed = pltpu.roll(column * back, lax.rem(total - group * local, total), 1)
    column_ref[...] = placed[:, :local]
    plan = jnp.exp2((row + column) - scores[...])
    return (plan * (1.0 / jnp.sum(plan, axis=0, keepdims=True))).astype(jnp.bfloat16)


def coupling_kernel(skipped, group_ref, scores, head_ref, rest_ref, moved_ref, row_ref, column_ref):
    local = column_ref.shape[1]
    weights = weigh(group_ref[0], local, scores, row_ref, column_ref)
    noise = jnp.concatenate(noise_of(head_ref, rest_ref, local, skipped), axis=1)
    moved = lax.dot_general(
        weights, noise, (((0,), (0,)), ((), ())), preferred_element_type=jnp.float32
    )
    moved_ref[...] = moved.astype(jnp.bfloat16).reshape(moved_ref.shape)


def blank_kernel(out_ref):
    pass


def blank(shape, dtype):
    return pl.pallas_call(
        blank_kernel, out_shape=jax.ShapeDtypeStruct(shape, dtype), out_specs=ANY
    )()


def per_device(latents, noise):
    local, channels, width = latents.shape
    dp, seq, near = lax.axis_size(DP), lax.axis_size(SEQ), lax.axis_size(NEAR)
    total = local * dp
    factor = math.log2(math.e) / (BLUR * math.sqrt(channels * width * seq))
    group = lax.axis_index(DP).reshape(1).astype(jnp.int32)

    head = local // 2
    upper = lax.axis_index("c") == 1

    square = (total, total)

    tail = (dp, PARTS * local - head, width // PARTS)

    def pair_terms(clips, tails=0):
        return pl.pallas_call(
            functools.partial(pair_kernel, factor),
            out_shape=(jax.ShapeDtypeStruct(square, jnp.float32),)
            + (jax.ShapeDtypeStruct(tail, noise.dtype),) * tails,
            in_specs=[VMEM, VMEM],
            out_specs=(VMEM,) * (1 + tails),
            compiler_params=LIMIT,
        )(*clips)

    def start_upper(noise, latents):
        first, second = pack(noise, latents, (head, 2 * PARTS * local - head))
        first, second, unused = lax.optimization_barrier((first, second, blank(square, jnp.float32)))
        first, second = lax.optimization_barrier((exchange(first, DP), second))
        return first, second, unused

    def start_lower(noise, latents):
        (packed,) = pack(noise, latents, (2 * PARTS * local,))
        clips = exchange(packed, DP)
        clips = clips[:, :head], clips[:, head:]
        return *clips, *pair_terms(clips)

    def finish_upper(first, second):
        return pair_terms((first, exchange(second, DP)), tails=1)

    def finish_lower(first, second):
        return blank(square, jnp.float32), blank(tail, noise.dtype)

    first, second, terms = lax.cond(upper, start_upper, start_lower, noise, latents)
    received = lax.ppermute(terms, "c", [(0, 1)])
    upper_terms, upper_noise = lax.cond(upper, finish_upper, finish_lower, first, second)

    def reduce_cost(terms, received):
        summed = terms + received
        parts = exchange(summed.reshape(near, total // near, total), NEAR)
        parts = exchange(spread(parts, lax.axis_size("h")), "h")
        parts = exchange(spread(parts, lax.axis_size("q")), "q")
        return exchange(spread(parts, near), NEAR).reshape(total, total)

    def move(skipped, cost, clips, group):
        moved, row, column = pl.pallas_call(
            functools.partial(coupling_kernel, skipped),
            out_shape=(jax.ShapeDtypeStruct((dp, local, width), noise.dtype), *ends),
            in_specs=[SMEM, VMEM, VMEM, VMEM],
            out_specs=(VMEM, VMEM, VMEM),
            compiler_params=LIMIT,
        )(group, cost, *clips)
        return exchange(moved, DP), row, column

    ends = (jax.ShapeDtypeStruct((1, total), jnp.float32), jax.ShapeDtypeStruct((1, local), jnp.float32))
    cost = lax.cond(
        upper, reduce_cost, lambda terms, received: blank(square, jnp.float32), upper_terms, received
    )
    sent = lax.ppermute(cost, "c", [(1, 0)])
    done = lax.cond(
        upper,
        functools.partial(move, 0),
        lambda cost, clips, group: (blank((dp, local, width), noise.dtype), *(blank(e.shape, e.dtype) for e in ends)),
        cost,
        (first, upper_noise),
        group,
    )
    targets, row, column = lax.cond(
        upper,
        lambda done, sent, clips, group: done,
        lambda done, sent, clips, group: move(local, sent, clips, group),
        done,
        sent,
        (first, second),
        group,
    )
    return (targets.swapaxes(0, 1), row.reshape(total), column.reshape(local))


def solution(mesh):
    fine = Mesh(mesh.devices.reshape(tuple(FINE.values())), tuple(FINE))
    in_specs = (P(DP, None, SEQ), P(DP, None, SEQ))
    out_specs = (P(DP, None, SEQ), P(), P(DP))
    return jax.shard_map(
        per_device, mesh=fine, in_specs=in_specs, out_specs=out_specs, check_vma=False
    )
```

```python
import functools
import math

import jax
import jax.numpy as jnp
from jax import lax
from jax.experimental import pallas as pl
from jax.experimental.pallas import tpu as pltpu
from jax.sharding import Mesh, PartitionSpec as P

ITERS = 4
PARTS = 2
BLUR = 0.5
FINE = {"z": 2, "q": 4, "p": 2, "h": 4, "x": 4, "c": 2}
DP = ("z", "q", "p")
SEQ = ("h", "x", "c")
NEAR = ("x", "z", "p")
ANY = pl.BlockSpec(memory_space=pl.ANY)
HBM = pl.BlockSpec(memory_space=pltpu.HBM)
VMEM = pl.BlockSpec(memory_space=pltpu.VMEM)
SMEM = pl.BlockSpec(memory_space=pltpu.SMEM)
LIMIT = pltpu.CompilerParams(vmem_limit_bytes=32 * 1024 * 1024)


def pack_kernel(noise_ref, latents_ref, *rest):
    *out_refs, held, arrived = rest
    local, _, width = noise_ref.shape
    width //= PARTS
    copies = [
        pltpu.make_async_copy(given, held.at[k], arrived.at[k])
        for k, given in enumerate((noise_ref, latents_ref))
    ]
    for copy in copies:
        copy.start()
    for k, copy in enumerate(copies):
        copy.wait()
        turned = jnp.swapaxes(held[k], 0, 1)
        for part in range(PARTS):
            start = (part * 2 + k) * local
            piece = turned[:, :, part * width : (part + 1) * width]
            first = 0
            for out_ref in out_refs:
                last = first + out_ref.shape[1]
                low, high = max(first, start), min(last, start + local)
                if low < high:
                    out_ref[:, low - first : high - first, :] = piece[:, low - start : high - start, :]
                first = last


def pack(noise, latents, runs):
    local, channels, width = noise.shape
    return pl.pallas_call(
        pack_kernel,
        out_shape=tuple(jax.ShapeDtypeStruct((channels, rows, width // PARTS), noise.dtype) for rows in runs),
        in_specs=[HBM, HBM],
        out_specs=(VMEM,) * len(runs),
        scratch_shapes=[
            pltpu.VMEM((2, *noise.shape), noise.dtype),
            pltpu.SemaphoreType.DMA((2,)),
        ],
        compiler_params=LIMIT,
    )(*(pltpu.with_memory_space_constraint(given, pltpu.HBM) for given in (noise, latents)))


def noise_of(head_ref, rest_ref, local, skipped):
    sources, head, width = head_ref.shape
    tail = local - head
    parts = [jnp.concatenate([head_ref[...], rest_ref[:, :tail, :]], axis=1)]
    for part in range(1, PARTS):
        first = tail + skipped + (part - 1) * (local + skipped)
        parts.append(rest_ref[:, first : first + local, :])
    return [part.reshape(sources * local, width) for part in parts]


def square_sums(parts):
    total = 0.0
    for part in parts:
        wide = part.astype(jnp.float32)
        total += wide * wide
    return jnp.sum(total, axis=1, keepdims=True)


def pair_kernel(factor, head_ref, rest_ref, out_ref, *tail_refs):
    sources, head, width = head_ref.shape
    local = (head + rest_ref.shape[1]) // (2 * PARTS)
    total = sources * local
    tail = local - head
    noises = noise_of(head_ref, rest_ref, local, local)
    latents = [
        rest_ref[:, first : first + local, :].reshape(total, width)
        for first in range(tail, rest_ref.shape[1], 2 * local)
    ]
    noise_norms = square_sums(noises) * factor
    latent_norms = square_sums(latents) * factor
    latent_norms = jnp.transpose(jnp.broadcast_to(latent_norms, (total, 128)))[:1, :]
    cross = lax.dot_general(
        jnp.concatenate(noises, axis=1),
        jnp.concatenate(latents, axis=1),
        (((1,), (1,)), ((), ())),
        preferred_element_type=jnp.float32,
    )
    out_ref[...] = noise_norms + latent_norms - (2.0 * factor) * cross
    for tail_ref in tail_refs:
        tail_ref[:, :tail, :] = rest_ref[:, :tail, :]
        for part in range(1, PARTS):
            first = tail + local + (part - 1) * 2 * local
            to = tail + (part - 1) * local
            tail_ref[:, to : to + local, :] = rest_ref[:, first : first + local, :]


def spread_kernel(parts_ref, out_ref):
    out_ref[...] = jnp.broadcast_to(jnp.sum(parts_ref[...], axis=0)[None], out_ref.shape)


def spread(parts, copies):
    return pl.pallas_call(
        spread_kernel,
        out_shape=jax.ShapeDtypeStruct((copies, *parts.shape[1:]), parts.dtype),
        in_specs=[VMEM],
        out_specs=VMEM,
        compiler_params=LIMIT,
    )(parts)


def exchange(blocks, axes):
    return lax.all_to_all(blocks, axes, 0, 0, tiled=True)


def weigh(group, local, scores, row_ref, column_ref):
    total = scores.shape[0]
    log_mass = -math.log2(total)
    row = jnp.zeros((total, 1), jnp.float32)
    for step in range(ITERS):
        value = row - scores[...]
        top = jnp.max(value, axis=0, keepdims=True)
        mass = jnp.sum(jnp.exp2(value - top), axis=0, keepdims=True)
        column = log_mass - (top + jnp.log2(mass))
        value = column - scores[...]
        top = jnp.max(value, axis=1, keepdims=True)
        mass = jnp.sum(jnp.exp2(value - top), axis=1, keepdims=True)
        row = log_mass - (top + jnp.log2(mass))
    back = BLUR * math.log(2.0)
    row_ref[...] = jnp.transpose(jnp.broadcast_to(row * back, (total, 128)))[:1, :]
    placed = pltpu.roll(column * back, lax.rem(total - group * local, total), 1)
    column_ref[...] = placed[:, :local]
    plan = jnp.exp2((row + column) - scores[...])
    return (plan * (1.0 / jnp.sum(plan, axis=0, keepdims=True))).astype(jnp.bfloat16)


def coupling_kernel(skipped, group_ref, scores, head_ref, rest_ref, moved_ref, row_ref, column_ref):
    local = column_ref.shape[1]
    weights = weigh(group_ref[0], local, scores, row_ref, column_ref)
    noise = jnp.concatenate(noise_of(head_ref, rest_ref, local, skipped), axis=1)
    moved = lax.dot_general(
        weights, noise, (((0,), (0,)), ((), ())), preferred_element_type=jnp.float32
    )
    moved_ref[...] = moved.astype(jnp.bfloat16).reshape(moved_ref.shape)


def blank_kernel(out_ref):
    pass


def blank(shape, dtype):
    return pl.pallas_call(
        blank_kernel, out_shape=jax.ShapeDtypeStruct(shape, dtype), out_specs=ANY
    )()


def per_device(latents, noise):
    local, channels, width = latents.shape
    dp, seq, near = lax.axis_size(DP), lax.axis_size(SEQ), lax.axis_size(NEAR)
    total = local * dp
    factor = math.log2(math.e) / (BLUR * math.sqrt(channels * width * seq))
    group = lax.axis_index(DP).reshape(1).astype(jnp.int32)

    head = local // 2
    upper = lax.axis_index("c") == 1

    square = (total, total)

    tail = (dp, PARTS * local - head, width // PARTS)

    def pair_terms(clips, tails=0):
        return pl.pallas_call(
            functools.partial(pair_kernel, factor),
            out_shape=(jax.ShapeDtypeStruct(square, jnp.float32),)
            + (jax.ShapeDtypeStruct(tail, noise.dtype),) * tails,
            in_specs=[VMEM, VMEM],
            out_specs=(VMEM,) * (1 + tails),
            compiler_params=LIMIT,
        )(*clips)

    def start_upper(noise, latents):
        first, second = pack(noise, latents, (head, 2 * PARTS * local - head))
        first, second, unused = lax.optimization_barrier((first, second, blank(square, jnp.float32)))
        first, second = lax.optimization_barrier((exchange(first, DP), second))
        return first, second, unused

    def start_lower(noise, latents):
        (packed,) = pack(noise, latents, (2 * PARTS * local,))
        clips = exchange(packed, DP)
        clips = clips[:, :head], clips[:, head:]
        return *clips, *pair_terms(clips)

    def finish_upper(first, second):
        return pair_terms((first, exchange(second, DP)), tails=1)

    def finish_lower(first, second):
        return blank(square, jnp.float32), blank(tail, noise.dtype)

    first, second, terms = lax.cond(upper, start_upper, start_lower, noise, latents)
    received = lax.ppermute(terms, "c", [(0, 1)])
    upper_terms, upper_noise = lax.cond(upper, finish_upper, finish_lower, first, second)

    def reduce_cost(terms, received):
        summed = terms + received
        parts = exchange(summed.reshape(near, total // near, total), NEAR)
        parts = exchange(spread(parts, lax.axis_size("q")), "q")
        parts = exchange(spread(parts, lax.axis_size("h")), "h")
        return exchange(spread(parts, near), NEAR).reshape(total, total)

    def move(skipped, cost, clips, group):
        moved, row, column = pl.pallas_call(
            functools.partial(coupling_kernel, skipped),
            out_shape=(jax.ShapeDtypeStruct((dp, local, width), noise.dtype), *ends),
            in_specs=[SMEM, VMEM, VMEM, VMEM],
            out_specs=(VMEM, VMEM, VMEM),
            compiler_params=LIMIT,
        )(group, cost, *clips)
        return exchange(moved, DP), row, column

    ends = (jax.ShapeDtypeStruct((1, total), jnp.float32), jax.ShapeDtypeStruct((1, local), jnp.float32))
    cost = lax.cond(
        upper, reduce_cost, lambda terms, received: blank(square, jnp.float32), upper_terms, received
    )
    sent = lax.ppermute(cost, "c", [(1, 0)])
    done = lax.cond(
        upper,
        functools.partial(move, 0),
        lambda cost, clips, group: (blank((dp, local, width), noise.dtype), *(blank(e.shape, e.dtype) for e in ends)),
        cost,
        (first, upper_noise),
        group,
    )
    targets, row, column = lax.cond(
        upper,
        lambda done, sent, clips, group: done,
        lambda done, sent, clips, group: move(local, sent, clips, group),
        done,
        sent,
        (first, second),
        group,
    )
    return (targets.swapaxes(0, 1), row.reshape(total), column.reshape(local))


def solution(mesh):
    fine = Mesh(mesh.devices.reshape(tuple(FINE.values())), tuple(FINE))
    in_specs = (P(DP, None, SEQ), P(DP, None, SEQ))
    out_specs = (P(DP, None, SEQ), P(), P(DP))
    return jax.shard_map(
        per_device, mesh=fine, in_specs=in_specs, out_specs=out_specs, check_vma=False
    )
```

```python
import functools
import math

import jax
import jax.numpy as jnp
from jax import lax
from jax.experimental import pallas as pl
from jax.experimental.pallas import tpu as pltpu
from jax.sharding import Mesh, PartitionSpec as P

ITERS = 4
PARTS = 2
BLUR = 0.5
FINE = {"z": 2, "q": 4, "p": 2, "h": 4, "x": 4, "c": 2}
DP = ("z", "q", "p")
SEQ = ("h", "x", "c")
NEAR = ("x", "z", "p")
ANY = pl.BlockSpec(memory_space=pl.ANY)
HBM = pl.BlockSpec(memory_space=pltpu.HBM)
VMEM = pl.BlockSpec(memory_space=pltpu.VMEM)
SMEM = pl.BlockSpec(memory_space=pltpu.SMEM)
LIMIT = pltpu.CompilerParams(vmem_limit_bytes=32 * 1024 * 1024)


def pack_kernel(noise_ref, latents_ref, *rest):
    *out_refs, held, arrived = rest
    local, _, width = noise_ref.shape
    width //= PARTS
    copies = [
        pltpu.make_async_copy(given, held.at[k], arrived.at[k])
        for k, given in enumerate((noise_ref, latents_ref))
    ]
    for copy in copies:
        copy.start()
    for k, copy in enumerate(copies):
        copy.wait()
        turned = jnp.swapaxes(held[k], 0, 1)
        for part in range(PARTS):
            start = (part * 2 + k) * local
            piece = turned[:, :, part * width : (part + 1) * width]
            first = 0
            for out_ref in out_refs:
                last = first + out_ref.shape[1]
                low, high = max(first, start), min(last, start + local)
                if low < high:
                    out_ref[:, low - first : high - first, :] = piece[:, low - start : high - start, :]
                first = last


def pack(noise, latents, runs):
    local, channels, width = noise.shape
    return pl.pallas_call(
        pack_kernel,
        out_shape=tuple(jax.ShapeDtypeStruct((channels, rows, width // PARTS), noise.dtype) for rows in runs),
        in_specs=[HBM, HBM],
        out_specs=(VMEM,) * len(runs),
        scratch_shapes=[
            pltpu.VMEM((2, *noise.shape), noise.dtype),
            pltpu.SemaphoreType.DMA((2,)),
        ],
        compiler_params=LIMIT,
    )(*(pltpu.with_memory_space_constraint(given, pltpu.HBM) for given in (noise, latents)))


def unpack_kernel(moved_ref, out_ref, held, written):
    half = moved_ref.shape[1] // 2
    copies = []
    for k in range(2):
        clips = pl.ds(k * half, half)
        held[clips] = jnp.swapaxes(moved_ref[:, clips, :], 0, 1)
        copies.append(pltpu.make_async_copy(held.at[clips], out_ref.at[clips], written.at[k]))
        copies[k].start()
    for copy in copies:
        copy.wait()


def unpack(moved):
    channels, local, width = moved.shape
    shape = (local, channels, width)
    return pl.pallas_call(
        unpack_kernel,
        out_shape=jax.ShapeDtypeStruct(shape, moved.dtype),
        in_specs=[VMEM],
        out_specs=ANY,
        scratch_shapes=[pltpu.VMEM(shape, moved.dtype), pltpu.SemaphoreType.DMA((2,))],
        compiler_params=LIMIT,
    )(moved)


def noise_of(head_ref, rest_ref, local, skipped):
    sources, head, width = head_ref.shape
    tail = local - head
    parts = [jnp.concatenate([head_ref[...], rest_ref[:, :tail, :]], axis=1)]
    for part in range(1, PARTS):
        first = tail + skipped + (part - 1) * (local + skipped)
        parts.append(rest_ref[:, first : first + local, :])
    return [part.reshape(sources * local, width) for part in parts]


def square_sums(parts):
    total = 0.0
    for part in parts:
        wide = part.astype(jnp.float32)
        total += wide * wide
    return jnp.sum(total, axis=1, keepdims=True)


def pair_kernel(factor, head_ref, rest_ref, out_ref, *tail_refs):
    sources, head, width = head_ref.shape
    local = (head + rest_ref.shape[1]) // (2 * PARTS)
    total = sources * local
    tail = local - head
    noises = noise_of(head_ref, rest_ref, local, local)
    latents = [
        rest_ref[:, first : first + local, :].reshape(total, width)
        for first in range(tail, rest_ref.shape[1], 2 * local)
    ]
    noise_norms = square_sums(noises) * factor
    latent_norms = square_sums(latents) * factor
    latent_norms = jnp.transpose(jnp.broadcast_to(latent_norms, (total, 128)))[:1, :]
    cross = lax.dot_general(
        jnp.concatenate(noises, axis=1),
        jnp.concatenate(latents, axis=1),
        (((1,), (1,)), ((), ())),
        preferred_element_type=jnp.float32,
    )
    out_ref[...] = noise_norms + latent_norms - (2.0 * factor) * cross
    for tail_ref in tail_refs:
        tail_ref[:, :tail, :] = rest_ref[:, :tail, :]
        for part in range(1, PARTS):
            first = tail + local + (part - 1) * 2 * local
            to = tail + (part - 1) * local
            tail_ref[:, to : to + local, :] = rest_ref[:, first : first + local, :]


def spread_kernel(parts_ref, out_ref):
    out_ref[...] = jnp.broadcast_to(jnp.sum(parts_ref[...], axis=0)[None], out_ref.shape)


def spread(parts, copies):
    return pl.pallas_call(
        spread_kernel,
        out_shape=jax.ShapeDtypeStruct((copies, *parts.shape[1:]), parts.dtype),
        in_specs=[VMEM],
        out_specs=VMEM,
        compiler_params=LIMIT,
    )(parts)


def exchange(blocks, axes):
    return lax.all_to_all(blocks, axes, 0, 0, tiled=True)


def weigh(group, local, scores, row_ref, column_ref):
    total = scores.shape[0]
    log_mass = -math.log2(total)
    row = jnp.zeros((total, 1), jnp.float32)
    for step in range(ITERS):
        value = row - scores[...]
        top = jnp.max(value, axis=0, keepdims=True)
        mass = jnp.sum(jnp.exp2(value - top), axis=0, keepdims=True)
        column = log_mass - (top + jnp.log2(mass))
        value = column - scores[...]
        top = jnp.max(value, axis=1, keepdims=True)
        mass = jnp.sum(jnp.exp2(value - top), axis=1, keepdims=True)
        row = log_mass - (top + jnp.log2(mass))
    back = BLUR * math.log(2.0)
    row_ref[...] = jnp.transpose(jnp.broadcast_to(row * back, (total, 128)))[:1, :]
    placed = pltpu.roll(column * back, lax.rem(total - group * local, total), 1)
    column_ref[...] = placed[:, :local]
    plan = jnp.exp2((row + column) - scores[...])
    return (plan * (1.0 / jnp.sum(plan, axis=0, keepdims=True))).astype(jnp.bfloat16)


def coupling_kernel(skipped, group_ref, scores, head_ref, rest_ref, moved_ref, row_ref, column_ref):
    local = column_ref.shape[1]
    weights = weigh(group_ref[0], local, scores, row_ref, column_ref)
    noise = jnp.concatenate(noise_of(head_ref, rest_ref, local, skipped), axis=1)
    moved = lax.dot_general(
        weights, noise, (((0,), (0,)), ((), ())), preferred_element_type=jnp.float32
    )
    moved_ref[...] = moved.astype(jnp.bfloat16).reshape(moved_ref.shape)


def blank_kernel(out_ref):
    pass


def blank(shape, dtype):
    return pl.pallas_call(
        blank_kernel, out_shape=jax.ShapeDtypeStruct(shape, dtype), out_specs=ANY
    )()


def per_device(latents, noise):
    local, channels, width = latents.shape
    dp, seq, near = lax.axis_size(DP), lax.axis_size(SEQ), lax.axis_size(NEAR)
    total = local * dp
    factor = math.log2(math.e) / (BLUR * math.sqrt(channels * width * seq))
    group = lax.axis_index(DP).reshape(1).astype(jnp.int32)

    head = local // 2
    upper = lax.axis_index("c") == 1

    square = (total, total)

    tail = (dp, PARTS * local - head, width // PARTS)

    def pair_terms(clips, tails=0):
        return pl.pallas_call(
            functools.partial(pair_kernel, factor),
            out_shape=(jax.ShapeDtypeStruct(square, jnp.float32),)
            + (jax.ShapeDtypeStruct(tail, noise.dtype),) * tails,
            in_specs=[VMEM, VMEM],
            out_specs=(VMEM,) * (1 + tails),
            compiler_params=LIMIT,
        )(*clips)

    def start_upper(noise, latents):
        first, second = pack(noise, latents, (head, 2 * PARTS * local - head))
        first, second, unused = lax.optimization_barrier((first, second, blank(square, jnp.float32)))
        first, second = lax.optimization_barrier((exchange(first, DP), second))
        return first, second, unused

    def start_lower(noise, latents):
        (packed,) = pack(noise, latents, (2 * PARTS * local,))
        clips = exchange(packed, DP)
        clips = clips[:, :head], clips[:, head:]
        return *clips, *pair_terms(clips)

    def finish_upper(first, second):
        return pair_terms((first, exchange(second, DP)), tails=1)

    def finish_lower(first, second):
        return blank(square, jnp.float32), blank(tail, noise.dtype)

    first, second, terms = lax.cond(upper, start_upper, start_lower, noise, latents)
    received = lax.ppermute(terms, "c", [(0, 1)])
    upper_terms, upper_noise = lax.cond(upper, finish_upper, finish_lower, first, second)

    def reduce_cost(terms, received):
        summed = terms + received
        parts = exchange(summed.reshape(near, total // near, total), NEAR)
        parts = exchange(spread(parts, lax.axis_size("h")), "h")
        parts = exchange(spread(parts, lax.axis_size("q")), "q")
        return exchange(spread(parts, near), NEAR).reshape(total, total)

    def move(skipped, cost, clips, group):
        moved, row, column = pl.pallas_call(
            functools.partial(coupling_kernel, skipped),
            out_shape=(jax.ShapeDtypeStruct((dp, local, width), noise.dtype), *ends),
            in_specs=[SMEM, VMEM, VMEM, VMEM],
            out_specs=(VMEM, VMEM, VMEM),
            compiler_params=LIMIT,
        )(group, cost, *clips)
        return exchange(moved, DP), row, column

    ends = (jax.ShapeDtypeStruct((1, total), jnp.float32), jax.ShapeDtypeStruct((1, local), jnp.float32))
    cost = lax.cond(
        upper, reduce_cost, lambda terms, received: blank(square, jnp.float32), upper_terms, received
    )
    sent = lax.ppermute(cost, "c", [(1, 0)])
    done = lax.cond(
        upper,
        functools.partial(move, 0),
        lambda cost, clips, group: (blank((dp, local, width), noise.dtype), *(blank(e.shape, e.dtype) for e in ends)),
        cost,
        (first, upper_noise),
        group,
    )
    targets, row, column = lax.cond(
        upper,
        lambda done, sent, clips, group: done,
        lambda done, sent, clips, group: move(local, sent, clips, group),
        done,
        sent,
        (first, second),
        group,
    )
    return (unpack(targets), row.reshape(total), column.reshape(local))


def solution(mesh):
    fine = Mesh(mesh.devices.reshape(tuple(FINE.values())), tuple(FINE))
    in_specs = (P(DP, None, SEQ), P(DP, None, SEQ))
    out_specs = (P(DP, None, SEQ), P(), P(DP))
    return jax.shard_map(
        per_device, mesh=fine, in_specs=in_specs, out_specs=out_specs, check_vma=False
    )
```

```python
import functools
import math

import jax
import jax.numpy as jnp
from jax import lax
from jax.experimental import pallas as pl
from jax.experimental.pallas import tpu as pltpu
from jax.sharding import Mesh, PartitionSpec as P

ITERS = 4
PARTS = 2
BLUR = 0.5
FINE = {"z": 2, "q": 4, "p": 2, "h": 4, "x": 4, "c": 2}
DP = ("z", "q", "p")
SEQ = ("h", "x", "c")
NEAR = ("x", "z", "p")
ANY = pl.BlockSpec(memory_space=pl.ANY)
HBM = pl.BlockSpec(memory_space=pltpu.HBM)
VMEM = pl.BlockSpec(memory_space=pltpu.VMEM)
SMEM = pl.BlockSpec(memory_space=pltpu.SMEM)
LIMIT = pltpu.CompilerParams(vmem_limit_bytes=12 * 1024 * 1024)


def pack_kernel(noise_ref, latents_ref, *rest):
    *out_refs, held, arrived = rest
    local, _, width = noise_ref.shape
    width //= PARTS
    copies = [
        pltpu.make_async_copy(given, held.at[k], arrived.at[k])
        for k, given in enumerate((noise_ref, latents_ref))
    ]
    for copy in copies:
        copy.start()
    for k, copy in enumerate(copies):
        copy.wait()
        turned = jnp.swapaxes(held[k], 0, 1)
        for part in range(PARTS):
            start = (part * 2 + k) * local
            piece = turned[:, :, part * width : (part + 1) * width]
            first = 0
            for out_ref in out_refs:
                last = first + out_ref.shape[1]
                low, high = max(first, start), min(last, start + local)
                if low < high:
                    out_ref[:, low - first : high - first, :] = piece[:, low - start : high - start, :]
                first = last


def pack(noise, latents, runs):
    local, channels, width = noise.shape
    return pl.pallas_call(
        pack_kernel,
        out_shape=tuple(jax.ShapeDtypeStruct((channels, rows, width // PARTS), noise.dtype) for rows in runs),
        in_specs=[HBM, HBM],
        out_specs=(VMEM,) * len(runs),
        scratch_shapes=[
            pltpu.VMEM((2, *noise.shape), noise.dtype),
            pltpu.SemaphoreType.DMA((2,)),
        ],
        compiler_params=LIMIT,
    )(*(pltpu.with_memory_space_constraint(given, pltpu.HBM) for given in (noise, latents)))


def noise_of(head_ref, rest_ref, local, skipped):
    sources, head, width = head_ref.shape
    tail = local - head
    parts = [jnp.concatenate([head_ref[...], rest_ref[:, :tail, :]], axis=1)]
    for part in range(1, PARTS):
        first = tail + skipped + (part - 1) * (local + skipped)
        parts.append(rest_ref[:, first : first + local, :])
    return [part.reshape(sources * local, width) for part in parts]


def square_sums(parts):
    total = 0.0
    for part in parts:
        wide = part.astype(jnp.float32)
        total += wide * wide
    return jnp.sum(total, axis=1, keepdims=True)


def pair_kernel(factor, head_ref, rest_ref, out_ref, *tail_refs):
    sources, head, width = head_ref.shape
    local = (head + rest_ref.shape[1]) // (2 * PARTS)
    total = sources * local
    tail = local - head
    noises = noise_of(head_ref, rest_ref, local, local)
    latents = [
        rest_ref[:, first : first + local, :].reshape(total, width)
        for first in range(tail, rest_ref.shape[1], 2 * local)
    ]
    noise_norms = square_sums(noises) * factor
    latent_norms = square_sums(latents) * factor
    latent_norms = jnp.transpose(jnp.broadcast_to(latent_norms, (total, 128)))[:1, :]
    cross = lax.dot_general(
        jnp.concatenate(noises, axis=1),
        jnp.concatenate(latents, axis=1),
        (((1,), (1,)), ((), ())),
        preferred_element_type=jnp.float32,
    )
    out_ref[...] = noise_norms + latent_norms - (2.0 * factor) * cross
    for tail_ref in tail_refs:
        tail_ref[:, :tail, :] = rest_ref[:, :tail, :]
        for part in range(1, PARTS):
            first = tail + local + (part - 1) * 2 * local
            to = tail + (part - 1) * local
            tail_ref[:, to : to + local, :] = rest_ref[:, first : first + local, :]


def spread_kernel(parts_ref, out_ref):
    out_ref[...] = jnp.broadcast_to(jnp.sum(parts_ref[...], axis=0)[None], out_ref.shape)


def spread(parts, copies):
    return pl.pallas_call(
        spread_kernel,
        out_shape=jax.ShapeDtypeStruct((copies, *parts.shape[1:]), parts.dtype),
        in_specs=[VMEM],
        out_specs=VMEM,
        compiler_params=LIMIT,
    )(parts)


def exchange(blocks, axes):
    return lax.all_to_all(blocks, axes, 0, 0, tiled=True)


def weigh(group, local, scores, row_ref, column_ref):
    total = scores.shape[0]
    log_mass = -math.log2(total)
    row = jnp.zeros((total, 1), jnp.float32)
    for step in range(ITERS):
        value = row - scores[...]
        top = jnp.max(value, axis=0, keepdims=True)
        mass = jnp.sum(jnp.exp2(value - top), axis=0, keepdims=True)
        column = log_mass - (top + jnp.log2(mass))
        value = column - scores[...]
        top = jnp.max(value, axis=1, keepdims=True)
        mass = jnp.sum(jnp.exp2(value - top), axis=1, keepdims=True)
        row = log_mass - (top + jnp.log2(mass))
    back = BLUR * math.log(2.0)
    row_ref[...] = jnp.transpose(jnp.broadcast_to(row * back, (total, 128)))[:1, :]
    placed = pltpu.roll(column * back, lax.rem(total - group * local, total), 1)
    column_ref[...] = placed[:, :local]
    plan = jnp.exp2((row + column) - scores[...])
    return (plan * (1.0 / jnp.sum(plan, axis=0, keepdims=True))).astype(jnp.bfloat16)


def coupling_kernel(skipped, group_ref, scores, head_ref, rest_ref, moved_ref, row_ref, column_ref):
    local = column_ref.shape[1]
    weights = weigh(group_ref[0], local, scores, row_ref, column_ref)
    noise = jnp.concatenate(noise_of(head_ref, rest_ref, local, skipped), axis=1)
    moved = lax.dot_general(
        weights, noise, (((0,), (0,)), ((), ())), preferred_element_type=jnp.float32
    )
    moved_ref[...] = moved.astype(jnp.bfloat16).reshape(moved_ref.shape)


def blank_kernel(out_ref):
    pass


def blank(shape, dtype):
    return pl.pallas_call(
        blank_kernel, out_shape=jax.ShapeDtypeStruct(shape, dtype), out_specs=ANY
    )()


def per_device(latents, noise):
    local, channels, width = latents.shape
    dp, seq, near = lax.axis_size(DP), lax.axis_size(SEQ), lax.axis_size(NEAR)
    total = local * dp
    factor = math.log2(math.e) / (BLUR * math.sqrt(channels * width * seq))
    group = lax.axis_index(DP).reshape(1).astype(jnp.int32)

    head = local // 2
    upper = lax.axis_index("c") == 1

    square = (total, total)

    tail = (dp, PARTS * local - head, width // PARTS)

    def pair_terms(clips, tails=0):
        return pl.pallas_call(
            functools.partial(pair_kernel, factor),
            out_shape=(jax.ShapeDtypeStruct(square, jnp.float32),)
            + (jax.ShapeDtypeStruct(tail, noise.dtype),) * tails,
            in_specs=[VMEM, VMEM],
            out_specs=(VMEM,) * (1 + tails),
            compiler_params=LIMIT,
        )(*clips)

    def start_upper(noise, latents):
        first, second = pack(noise, latents, (head, 2 * PARTS * local - head))
        first, second, unused = lax.optimization_barrier((first, second, blank(square, jnp.float32)))
        first, second = lax.optimization_barrier((exchange(first, DP), second))
        return first, second, unused

    def start_lower(noise, latents):
        (packed,) = pack(noise, latents, (2 * PARTS * local,))
        clips = exchange(packed, DP)
        clips = clips[:, :head], clips[:, head:]
        return *clips, *pair_terms(clips)

    def finish_upper(first, second):
        return pair_terms((first, exchange(second, DP)), tails=1)

    def finish_lower(first, second):
        return blank(square, jnp.float32), blank(tail, noise.dtype)

    first, second, terms = lax.cond(upper, start_upper, start_lower, noise, latents)
    received = lax.ppermute(terms, "c", [(0, 1)])
    upper_terms, upper_noise = lax.cond(upper, finish_upper, finish_lower, first, second)

    def reduce_cost(terms, received):
        summed = terms + received
        parts = exchange(summed.reshape(near, total // near, total), NEAR)
        parts = exchange(spread(parts, lax.axis_size("h")), "h")
        parts = exchange(spread(parts, lax.axis_size("q")), "q")
        return exchange(spread(parts, near), NEAR).reshape(total, total)

    def move(skipped, cost, clips, group):
        moved, row, column = pl.pallas_call(
            functools.partial(coupling_kernel, skipped),
            out_shape=(jax.ShapeDtypeStruct((dp, local, width), noise.dtype), *ends),
            in_specs=[SMEM, VMEM, VMEM, VMEM],
            out_specs=(VMEM, VMEM, VMEM),
            compiler_params=LIMIT,
        )(group, cost, *clips)
        return exchange(moved, DP), row, column

    ends = (jax.ShapeDtypeStruct((1, total), jnp.float32), jax.ShapeDtypeStruct((1, local), jnp.float32))
    cost = lax.cond(
        upper, reduce_cost, lambda terms, received: blank(square, jnp.float32), upper_terms, received
    )
    sent = lax.ppermute(cost, "c", [(1, 0)])
    done = lax.cond(
        upper,
        functools.partial(move, 0),
        lambda cost, clips, group: (blank((dp, local, width), noise.dtype), *(blank(e.shape, e.dtype) for e in ends)),
        cost,
        (first, upper_noise),
        group,
    )
    targets, row, column = lax.cond(
        upper,
        lambda done, sent, clips, group: done,
        lambda done, sent, clips, group: move(local, sent, clips, group),
        done,
        sent,
        (first, second),
        group,
    )
    return (targets.swapaxes(0, 1), row.reshape(total), column.reshape(local))


def solution(mesh):
    fine = Mesh(mesh.devices.reshape(tuple(FINE.values())), tuple(FINE))
    in_specs = (P(DP, None, SEQ), P(DP, None, SEQ))
    out_specs = (P(DP, None, SEQ), P(), P(DP))
    return jax.shard_map(
        per_device, mesh=fine, in_specs=in_specs, out_specs=out_specs, check_vma=False
    )
```
